512 devices in a mesh: row: 16 (over z_lo, x), col: 32 (over z_hi, y, core).
Axes of the slice: x: 4, y: 4, z: 16 (z_hi: 4, z_lo: 4; z = z_hi * 4 + z_lo), core: 2. Of those that a mesh axis runs over, the one named last changes fastest.
Arguments:
- features: bfloat16 [65536, 256], P(('col', 'row')), may hold values from -6 to 6
- weight: bfloat16 [256, 256], replicated, may hold values from -0.375 to 0.375
- tile_values: bfloat16 [16, 32, 128, 128, 128], P('row', 'col'), as said below
- tile_rows: int32 [16, 32, 128], P('row', 'col'), may hold values from 0 to 31, as said below
- tile_cols: int32 [16, 32, 128], P('row', 'col'), may hold values from 0 to 15, as said below
- tile_count: int32 [16, 32], P('row', 'col'), may hold values from 16 to 128, as said below
- cotangent: bfloat16 [65536, 256], P(('row', 'col')), may hold values from -6 to 6
Outputs:
- activated: bfloat16 [65536, 256], P(('row', 'col'))
- grad_features: bfloat16 [65536, 256], P(('col', 'row'))
- grad_weight: float32 [256, 256], replicated
The draws below stay inside these ranges and needn't reach their ends.
Inputs may be any that keep to these rules, and one draw needn't show every extreme that they name: `tile_count`: the number of live slots of each block: its slots below this number hold the block's nonzero tiles, the others are padding; at least one block has exactly 128. `tile_rows`: the 128 slots of one block name distinct (tile row, tile column) pairs. `tile_cols`: the 128 slots of one block name distinct (tile row, tile column) pairs. `tile_values`: edge weights are nonnegative; most entries of a tile are zero.
All inputs are finite; a program needn't handle non-finite values.
Results may differ from the reference program's by a relative error of at most 0.028.
Values may be sent and summed in bfloat16 or wider, within the bound.
No kernel may reach another device: no remote copies, remote signals or barrier semaphores. Data moves between devices by JAX's collectives and lax.ppermute only.
A program may use at most 64 MiB of HBM per device.

```python
import math
import jax
import jax.numpy as jnp
from jax import lax

WIDTH = 256
TILE = 128
ROW_BLOCKS = 16
COL_BLOCKS = 32
NODES = 65536
ROW_TILES = 32
COL_TILES = 16
SLOTS = 128


def tile_positions(key):
    block_keys = jax.random.split(key, ROW_BLOCKS * COL_BLOCKS)

    def one_block(block_key):
        return jax.random.permutation(block_key, ROW_TILES * COL_TILES)[:SLOTS]
    chosen = jax.vmap(one_block)(block_keys)
    return chosen.reshape(ROW_BLOCKS, COL_BLOCKS, SLOTS).astype(jnp.int32)


def draw_tile_rows(key, part):
    return (tile_positions(key) // COL_TILES).astype(jnp.int32)


def draw_tile_cols(key, part):
    return (tile_positions(key) % COL_TILES).astype(jnp.int32)


def sparse_weights(key, low_value, high_value):
    mask_key, value_key = jax.random.split(key)
    shape = (ROW_BLOCKS, COL_BLOCKS, SLOTS, TILE, TILE)
    density = max(0.125, 4.0 / TILE)
    present = jax.random.bernoulli(mask_key, density, shape).astype(jnp.float32)
    magnitude = jax.random.uniform(value_key, shape, jnp.float32, low_value, high_value)
    per_row = COL_BLOCKS * (SLOTS / ROW_TILES) * TILE * density
    return present * magnitude * (1.0 / per_row ** 0.5)


def draw_tile_values(key, part):
    key = jax.random.fold_in(key, 11)
    values = sparse_weights(key, 0.5, 1.5)
    return values.astype(jnp.bfloat16)


def draw_tile_count(key, part):
    key = jax.random.fold_in(key, 7)
    light_key, heavy_key = jax.random.split(key)
    block_total = ROW_BLOCKS * COL_BLOCKS
    lowest = max(1, SLOTS // 8)
    counts = jax.random.randint(light_key, (block_total,), lowest, SLOTS // 2 + 1)
    ranking = jax.random.permutation(heavy_key, block_total)
    heavy = ranking < max(1, block_total // 16)
    counts = jnp.where(heavy, SLOTS, counts)
    return counts.reshape(ROW_BLOCKS, COL_BLOCKS).astype(jnp.int32)


def block_scale(own_key, dims, shards, least, top_value):
    loudness, own = 1.0, jax.random.fold_in(own_key, 6)
    for position, shards_of in shards:
        steps = jnp.exp(jax.random.uniform(jax.random.fold_in(own, position), (shards_of,), jnp.float32, least / len(shards), top_value / len(shards)))
        loudness = loudness * jnp.repeat(steps, dims[position] // shards_of).reshape([-1 if axis == position else 1 for axis in range(len(dims))])
    return loudness


def normal_values(rng, shape, deviation, reach, pieces=(), kind=jnp.bfloat16):
    entries = jax.random.normal(rng, shape, jnp.float32) * deviation
    if len(pieces) > 0:
        entries = block_scale(rng, shape, pieces, -0.22, 0.18) * entries
    return jnp.clip(entries, min=-reach, max=reach).astype(kind)


def setup_inputs(seed: int = 0) -> dict:
    splits = jax.random.split(jax.random.key(seed), 8)
    features = normal_values(splits[0], (NODES, WIDTH), 1.0, 6.0, ((0, 512),))
    weight = normal_values(splits[1], (WIDTH, WIDTH), WIDTH ** -0.5, 0.375)
    tile_values = draw_tile_values(jax.random.fold_in(splits[7], 71), 0)
    tile_rows = draw_tile_rows(jax.random.fold_in(splits[7], 71), 0)
    tile_cols = draw_tile_cols(jax.random.fold_in(splits[7], 71), 0)
    tile_count = draw_tile_count(jax.random.fold_in(splits[7], 71), 0)
    cotangent = normal_values(splits[6], (NODES, WIDTH), 1.0, 6.0, ((0, 512),))
    return {"features": features, "weight": weight, "tile_values": tile_values, "tile_rows": tile_rows, "tile_cols": tile_cols, "tile_count": tile_count, "cotangent": cotangent}


def silu_slope(pre_act):
    sigmoid_part = jax.nn.sigmoid(pre_act)
    return sigmoid_part * (1.0 + pre_act * (1.0 - sigmoid_part))

def reference(features, weight, tile_values, tile_rows, tile_cols, tile_count, cotangent):
    block_total = ROW_BLOCKS * COL_BLOCKS
    all_values = tile_values.reshape(block_total, SLOTS, TILE, TILE)
    all_rows = tile_rows.reshape(block_total, SLOTS)
    all_cols = tile_cols.reshape(block_total, SLOTS)
    all_counts = tile_count.reshape(block_total)
    block_ids = jnp.arange(block_total, dtype=jnp.int32)
    slot_ids = jnp.arange(SLOTS, dtype=jnp.int32)
    row_ids = jnp.arange(ROW_TILES, dtype=jnp.int32)
    col_ids = jnp.arange(COL_TILES, dtype=jnp.int32)
    highest = lax.Precision.HIGHEST
    source = features.reshape(COL_BLOCKS, COL_TILES, TILE, WIDTH)

    def forward_block(running, item):
        block_id, block_values, block_rows, block_cols, live_count = item
        owner = block_id // COL_BLOCKS
        column = block_id % COL_BLOCKS
        in_use = (slot_ids < live_count).astype(jnp.float32)
        gathered = source[column][block_cols].astype(jnp.float32)
        products = jnp.einsum('smk,skf->smf', block_values.astype(jnp.float32), gathered, precision=highest)
        selector = (block_rows[:, None] == row_ids[None, :]).astype(jnp.float32) * in_use[:, None]
        block_sum = jnp.einsum('sr,smf->rmf', selector, products, precision=highest)
        rounded = lax.optimization_barrier(block_sum.astype(jnp.bfloat16)).astype(jnp.float32)
        return (running.at[owner].add(rounded), None)
    start_rows = jnp.zeros((ROW_BLOCKS, ROW_TILES, TILE, WIDTH), jnp.float32)
    summed, _ = lax.scan(forward_block, start_rows, (block_ids, all_values, all_rows, all_cols, all_counts))
    aggregated = summed.reshape(NODES, WIDTH).astype(jnp.bfloat16)
    pre_act = jnp.dot(aggregated, weight, preferred_element_type=jnp.float32)
    activated = jax.nn.silu(pre_act).astype(jnp.bfloat16)
    grad_pre = (cotangent.astype(jnp.float32) * silu_slope(pre_act)).astype(jnp.bfloat16)
    grad_weight = jnp.dot(aggregated.T, grad_pre, preferred_element_type=jnp.float32) * (1.0 / math.sqrt(NODES))
    target = grad_pre.reshape(ROW_BLOCKS, ROW_TILES, TILE, WIDTH)

    def backward_block(running, item):
        block_id, block_values, block_rows, block_cols, live_count = item
        owner = block_id // COL_BLOCKS
        column = block_id % COL_BLOCKS
        in_use = (slot_ids < live_count).astype(jnp.float32)
        gathered = target[owner][block_rows].astype(jnp.float32)
        products = jnp.einsum('smk,smf->skf', block_values.astype(jnp.float32), gathered, precision=highest)
        selector = (block_cols[:, None] == col_ids[None, :]).astype(jnp.float32) * in_use[:, None]
        block_sum = jnp.einsum('sc,skf->ckf', selector, products, precision=highest)
        return (running.at[column].add(block_sum), None)
    start_cols = jnp.zeros((COL_BLOCKS, COL_TILES, TILE, WIDTH), jnp.float32)
    back_sum, _ = lax.scan(backward_block, start_cols, (block_ids, all_values, all_rows, all_cols, all_counts))
    spread = back_sum.reshape(NODES, WIDTH).astype(jnp.bfloat16)
    grad_features = jnp.einsum('nk,fk->nf', spread, weight, preferred_element_type=jnp.float32).astype(jnp.bfloat16)
    return (activated, grad_features, grad_weight)
```

```python
import functools
import math

import jax
import jax.numpy as jnp
from jax import lax
from jax.experimental import pallas as pl
from jax.experimental.pallas import tpu as pltpu
from jax.sharding import PartitionSpec as P

TILE = 128
RING = 4
HALF = 16
UNROLL = 4
LIST = 192
VMEM_LIMIT = 24 * 1024 * 1024


def col_perm(move):
    pairs = []
    for c in range(32):
        zh, y, core = move(c // 8, (c // 2) % 4, c % 2)
        pairs.append((c, (zh % 4) * 8 + (y % 4) * 2 + core % 2))
    return pairs


def row_perm(move):
    pairs = []
    for r in range(16):
        zl, x = move(r // 4, r % 4)
        pairs.append((r, (zl % 4) * 4 + x % 4))
    return pairs


def send_zh(v, k):
    return lax.ppermute(v, "col", col_perm(lambda zh, y, c: (zh + k, y, c)))


def send_y(v, k):
    return lax.ppermute(v, "col", col_perm(lambda zh, y, c: (zh, y + k, c)))


def send_core(v):
    return lax.ppermute(v, "col", col_perm(lambda zh, y, c: (zh, y, c + 1)))


def send_zl(v, k):
    return lax.ppermute(v, "row", row_perm(lambda zl, x: (zl + k, x)))


def send_x(v, k):
    return lax.ppermute(v, "row", row_perm(lambda zl, x: (zl, x + k)))


def swap_zh(v, k):
    return lax.ppermute(v, "col", col_perm(lambda zh, y, c: (zh ^ k, y, c)))


def swap_y(v, k):
    return lax.ppermute(v, "col", col_perm(lambda zh, y, c: (zh, y ^ k, c)))


def swap_zl(v, k):
    return lax.ppermute(v, "row", row_perm(lambda zl, x: (zl ^ k, x)))


def swap_x(v, k):
    return lax.ppermute(v, "row", row_perm(lambda zl, x: (zl, x ^ k)))


def smem():
    return pl.BlockSpec(memory_space=pltpu.SMEM)


def vmem():
    return pl.BlockSpec(memory_space=pltpu.VMEM)


def plan_kernel(where, rows, cols, count, slots, sources, dests, groups, head, link):
    zl, x, zh, y, core = (where[i] for i in range(5))

    def clear(i, _):
        head[i] = -1
        return 0

    lax.fori_loop(0, 4 * HALF, clear, 0)

    def chain(s, _):
        r, c = rows[0, 0, s], cols[0, 0, s]
        mine = jnp.where((r & 1) == core, 1, 0)
        forward = mine * HALF + ((((r >> 1) & 3) - y) & 3) * 4 + (((r >> 3) - zh) & 3)
        backward = (3 - mine) * HALF + (((c & 3) - x) & 3) * 4 + (((c >> 2) - zl) & 3)
        link[0, s] = head[forward]
        head[forward] = s
        link[1, s] = head[backward]
        head[backward] = s
        return 0

    lax.fori_loop(0, count[0, 0], chain, 0)

    for q in range(4):
        way = q // 2

        def segment(d, pos, q=q, way=way):
            def more(state):
                return state[0] >= 0

            def emit(state):
                s, at = state
                r, c = rows[0, 0, s], cols[0, 0, s]
                if way == 0:
                    source = ((x - (c & 3)) & 3) * 4 + ((zl - (c >> 2)) & 3)
                else:
                    source = ((y - ((r >> 1) & 3)) & 3) * 4 + ((zh - (r >> 3)) & 3)
                slots[q, at] = s
                sources[q, at] = source
                dests[q, at >> 1] = d
                return link[way, s], at + 1

            _, at = lax.while_loop(more, emit, (head[q * HALF + d], pos))

            @pl.when((at & 1) == 1)
            def _():
                slots[q, at] = 0
                sources[q, at] = HALF

            return at + (at & 1)

        total = lax.fori_loop(0, HALF, segment, 0)

        for i in range(2 * UNROLL):
            slots[q, total + i] = 0
            sources[q, total + i] = HALF
            dests[q, (total >> 1) + (i >> 1)] = 0
        groups[q] = ((total >> 1) + UNROLL - 1) // UNROLL


def make_plan(where, rows, cols, count):
    i32 = jnp.int32
    return pl.pallas_call(
        plan_kernel,
        out_shape=(
            jax.ShapeDtypeStruct((4, LIST), i32),
            jax.ShapeDtypeStruct((4, LIST), i32),
            jax.ShapeDtypeStruct((4, LIST), i32),
            jax.ShapeDtypeStruct((4,), i32),
        ),
        in_specs=[smem()] * 4,
        out_specs=(smem(),) * 4,
        scratch_shapes=[pltpu.SMEM((4 * HALF,), i32), pltpu.SMEM((2, TILE), i32)],
        cost_estimate=pl.CostEstimate(flops=0, bytes_accessed=16 * 1024 * 1024, transcendentals=0),
        name="plan",
    )(where, rows, cols, count)


def turn_kernel(count, v, out):
    def step(i, _):
        for u in range(4):
            out[4 * i + u] = v[0, 0, 4 * i + u].T
        return 0

    lax.fori_loop(0, (count[0, 0] + 3) // 4, step, 0)


def turn_tiles(count, tile_values):
    return pl.pallas_call(
        turn_kernel,
        out_shape=jax.ShapeDtypeStruct(tile_values.shape[2:], tile_values.dtype),
        in_specs=[smem(), vmem()],
        out_specs=vmem(),
        compiler_params=pltpu.CompilerParams(vmem_limit_bytes=VMEM_LIMIT),
        cost_estimate=pl.CostEstimate(flops=0, bytes_accessed=24 * 1024 * 1024, transcendentals=0),
        name="turn",
    )(count, tile_values)


def spmm_kernel(q, has_start, slots, sources, dests, groups, v, s0, s1, s2, s3, *rest):
    if has_start:
        start, out, held, acc = rest
    else:
        out, held, acc = rest
    for k, part in enumerate((s0, s1, s2, s3)):
        held[RING * k : RING * (k + 1)] = part[...]
    held[HALF] = jnp.zeros_like(held[HALF])
    if has_start:
        acc[...] = start[...]
    else:
        acc[...] = jnp.zeros_like(acc)

    def step(g, _):
        products = []
        for u in range(UNROLL):
            at = (g * UNROLL + u) * 2
            left = jnp.concatenate([v[slots[q, at]], v[slots[q, at + 1]]], axis=1)
            right = jnp.concatenate([held[sources[q, at]], held[sources[q, at + 1]]], axis=0)
            products.append(jnp.dot(left, right, preferred_element_type=jnp.float32))
        for u in range(UNROLL):
            d = dests[q, g * UNROLL + u]
            acc[d] = acc[d] + products[u]
        return 0

    lax.fori_loop(0, groups[q], step, 0)
    out[...] = acc[...].astype(out.dtype)


def spmm(q, plan, v, parts, start=None, dtype=jnp.bfloat16):
    width = parts[0].shape[-1]
    extra = () if start is None else (start,)
    return pl.pallas_call(
        functools.partial(spmm_kernel, q, start is not None),
        out_shape=jax.ShapeDtypeStruct((HALF, TILE, width), dtype),
        in_specs=[smem()] * 4 + [vmem()] * (5 + len(extra)),
        out_specs=vmem(),
        scratch_shapes=[
            pltpu.VMEM((HALF + 1, TILE, width), jnp.bfloat16),
            pltpu.VMEM((HALF, TILE, width), jnp.float32),
        ],
        compiler_params=pltpu.CompilerParams(vmem_limit_bytes=VMEM_LIMIT),
        cost_estimate=pl.CostEstimate(
            flops=2 * 64 * TILE * TILE * width, bytes_accessed=12 * 1024 * 1024, transcendentals=0
        ),
        name="spmm",
    )(*plan, v, *parts, *extra)


def mid_kernel(a0, a1, a2, a3, w, cot, act_out, grad_out, part_out):
    f32 = jnp.float32
    total = a0[...].astype(f32) + a1[...].astype(f32) + a2[...].astype(f32) + a3[...].astype(f32)
    aggregated = total.astype(jnp.bfloat16)
    pre = jnp.dot(aggregated, w[...], preferred_element_type=f32)
    s = jax.nn.sigmoid(pre)
    act_out[...] = (pre * s).astype(jnp.bfloat16)
    grad = (cot[...].astype(f32) * (s * (1.0 + pre * (1.0 - s)))).astype(jnp.bfloat16)
    grad_out[...] = grad
    part_out[...] = lax.dot_general(
        aggregated, grad, (((0,), (0,)), ((), ())), preferred_element_type=f32
    )


def middle(parts, w, cot):
    n, width = cot.shape
    return pl.pallas_call(
        mid_kernel,
        out_shape=(
            jax.ShapeDtypeStruct((n, width), jnp.bfloat16),
            jax.ShapeDtypeStruct((n, width), jnp.bfloat16),
            jax.ShapeDtypeStruct((width, width), jnp.float32),
        ),
        compiler_params=pltpu.CompilerParams(vmem_limit_bytes=VMEM_LIMIT),
        name="middle",
    )(*parts, w, cot)


def last_kernel(a0, a1, a2, a3, w, out):
    f32 = jnp.float32
    total = a0[...].astype(f32) + a1[...].astype(f32) + a2[...].astype(f32) + a3[...].astype(f32)
    spread = total.astype(jnp.bfloat16)
    out[...] = lax.dot_general(
        spread, w[...], (((1,), (1,)), ((), ())), preferred_element_type=f32
    ).astype(jnp.bfloat16)


def last(parts, w):
    return pl.pallas_call(
        last_kernel,
        out_shape=jax.ShapeDtypeStruct(parts[0].shape, jnp.bfloat16),
        compiler_params=pltpu.CompilerParams(vmem_limit_bytes=VMEM_LIMIT),
        name="last",
    )(*parts, w)


def add4(a, b, c, d):
    f32 = jnp.float32
    return (a.astype(f32) + b.astype(f32) + c.astype(f32) + d.astype(f32)).astype(jnp.bfloat16)


def halve(part, bit, swap):
    low, high = jnp.split(part, 2, axis=0)
    keep = jnp.where(bit == 1, high, low)
    give = jnp.where(bit == 1, low, high)
    return keep + swap(give)


def join(part, bit, swap):
    other = swap(part)
    low = jnp.where(bit == 1, other, part)
    high = jnp.where(bit == 1, part, other)
    return jnp.concatenate([low, high], axis=0)


def total_over_all(part, x, y):
    xu, xv = (x ^ (x >> 1)) & 1, (x >> 1) & 1
    yu, yv = (y ^ (y >> 1)) & 1, (y >> 1) & 1
    part = halve(part, xu, lambda v: swap_x(v, 1))
    part = halve(part, xv, lambda v: swap_x(v, 3))
    part = halve(part, yu, lambda v: swap_y(v, 1))
    part = halve(part, yv, lambda v: swap_y(v, 3))
    part = part + swap_zl(part, 1)
    part = part + swap_zl(part, 2)
    part = part + send_core(part)
    part = part + swap_zh(part, 1)
    part = part + swap_zh(part, 3)
    part = join(part, yv, lambda v: swap_y(v, 3))
    part = join(part, yu, lambda v: swap_y(v, 1))
    part = join(part, xv, lambda v: swap_x(v, 3))
    return join(part, xu, lambda v: swap_x(v, 1))


def shards(features, weight, tile_values, tile_rows, tile_cols, tile_count, cotangent):
    node_dev, width = features.shape
    grad_scale = 1.0 / math.sqrt(node_dev * lax.axis_size("row") * lax.axis_size("col"))
    r, c = lax.axis_index("row"), lax.axis_index("col")
    zl, x, zh, y, core = r >> 2, r & 3, c >> 3, (c >> 1) & 3, c & 1
    where = jnp.stack([zl, x, zh, y, core]).astype(jnp.int32)
    tile = (1, node_dev, width)

    own = features.reshape(tile)
    line = jnp.concatenate([own] + [send_zl(own, k) for k in (1, 2, 3)], axis=0)
    source = [line] + [send_x(line, k) for k in (1, 2, 3)]
    plan = make_plan(where, tile_rows, tile_cols, tile_count)
    turned = turn_tiles(tile_count, tile_values)
    values = tile_values.reshape(tile_values.shape[2:])

    theirs = spmm(0, plan, values, source)
    got = send_core(theirs)
    mine = spmm(1, plan, values, source)
    paired = (mine.astype(jnp.float32) + got.astype(jnp.float32)).astype(jnp.bfloat16)
    blocks = [paired[4 * k : 4 * (k + 1)] for k in range(4)]
    blocks = add4(blocks[0], *[send_y(blocks[k], k) for k in (1, 2, 3)])
    pieces = [blocks[k] for k in range(4)]
    pieces = [pieces[0]] + [send_zh(pieces[k], k) for k in (1, 2, 3)]
    activated, grad_pre, weight_part = middle(pieces, weight, cotangent)

    own = grad_pre.reshape(tile)
    line = jnp.concatenate([own] + [send_zh(own, k) for k in (1, 2, 3)], axis=0)
    grads = [line] + [send_y(line, k) for k in (1, 2, 3)]
    other = send_core(jnp.concatenate(grads, axis=0))
    grad_weight = total_over_all(weight_part, x, y) * grad_scale

    first = spmm(2, plan, turned, grads, dtype=jnp.float32)
    others = [other[4 * k : 4 * (k + 1)] for k in range(4)]
    spread = spmm(3, plan, turned, others, start=first)
    blocks = [spread[4 * k : 4 * (k + 1)] for k in range(4)]
    blocks = add4(blocks[0], *[send_x(blocks[k], k) for k in (1, 2, 3)])
    pieces = [blocks[k] for k in range(4)]
    pieces = [pieces[0]] + [send_zl(pieces[k], k) for k in (1, 2, 3)]
    grad_features = last(pieces, weight)
    return (activated, grad_features, grad_weight)


def solution(mesh):
    return jax.shard_map(
        shards,
        mesh=mesh,
        in_specs=(
            P(("col", "row"), None),
            P(),
            P("row", "col", None, None, None),
            P("row", "col", None),
            P("row", "col", None),
            P("row", "col"),
            P(("row", "col"), None),
        ),
        out_specs=(P(("row", "col"), None), P(("col", "row"), None), P()),
        check_vma=False,
    )
```

```python
import functools
import math

import jax
import jax.numpy as jnp
from jax import lax
from jax.experimental import pallas as pl
from jax.experimental.pallas import tpu as pltpu
from jax.sharding import PartitionSpec as P

TILE = 128
ROWS = 16
COLS = 32
HALF = 16
GROUP = 8
UNROLL = 4
LIST = 192
VMEM_LIMIT = 24 * 1024 * 1024
BF16 = jnp.bfloat16
F32 = jnp.float32


def send_y(v, k):
    pairs = [(c, (c // 8) * 8 + ((c // 2 + k) % 4) * 2 + c % 2) for c in range(COLS)]
    return lax.ppermute(v, "col", pairs)


def send_core(v):
    return lax.ppermute(v, "col", [(c, c ^ 1) for c in range(COLS)])


def trade_row(v):
    return lax.all_to_all(v, "row", 0, 0)


def trade_zh(v):
    groups = [[zh * 8 + rest for zh in range(4)] for rest in range(8)]
    return lax.all_to_all(v, "col", 0, 0, axis_index_groups=groups)


def smem():
    return pl.BlockSpec(memory_space=pltpu.SMEM)


def vmem():
    return pl.BlockSpec(memory_space=pltpu.VMEM)


def params():
    return pltpu.CompilerParams(vmem_limit_bytes=VMEM_LIMIT)


def cost(flops, mib):
    return pl.CostEstimate(flops=flops, bytes_accessed=mib * 1024 * 1024, transcendentals=0)


def forward_kernel(where, rows, cols, count, v, xs, give, keep, acc):
    y, core = where[1], where[2]
    acc[...] = jnp.zeros_like(acc)
    live = count[0, 0]

    def step(g, _):
        products, dests = [], []
        for u in range(GROUP):
            s = g * GROUP + u
            r = rows[0, 0, s]
            mine = jnp.where((r & 1) == core, HALF, 0)
            d = mine + ((((r >> 1) & 3) - y) & 3) * 4 + (r >> 3)
            dests.append(jnp.where(s < live, d, 2 * HALF))
            products.append(
                jnp.dot(v[0, 0, s], xs[cols[0, 0, s]], preferred_element_type=F32)
            )
        for u in range(GROUP):
            acc[dests[u]] = acc[dests[u]] + products[u]
        return 0

    lax.fori_loop(0, (live + GROUP - 1) // GROUP, step, 0)
    give[...] = acc[:HALF].astype(BF16)
    keep[...] = acc[HALF : 2 * HALF].astype(BF16)


def forward(where, rows, cols, count, values, xs):
    width = xs.shape[-1]
    half = jax.ShapeDtypeStruct((HALF, TILE, width), BF16)
    return pl.pallas_call(
        forward_kernel,
        out_shape=(half, half),
        in_specs=[smem()] * 4 + [vmem()] * 2,
        out_specs=(vmem(), vmem()),
        scratch_shapes=[pltpu.VMEM((2 * HALF + 1, TILE, width), F32)],
        compiler_params=params(),
        cost_estimate=cost(2 * 128 * TILE * TILE * width, 7),
        name="forward",
    )(where, rows, cols, count, values, xs)


def plan_kernel(where, rows, cols, count, slots, sources, dests, groups, head, link):
    zh, y, core = where[0], where[1], where[2]

    def clear(i, _):
        head[i] = -1
        return 0

    lax.fori_loop(0, 2 * HALF, clear, 0)

    def chain(s, _):
        r, c = rows[0, 0, s], cols[0, 0, s]
        at = jnp.where((r & 1) == core, 0, HALF) + c
        link[s] = head[at]
        head[at] = s
        return 0

    lax.fori_loop(0, count[0, 0], chain, 0)

    for q in range(2):

        def segment(d, pos, q=q):
            def more(state):
                return state[0] >= 0

            def emit(state):
                s, at = state
                r = rows[0, 0, s]
                slots[q, at] = s
                sources[q, at] = ((y - ((r >> 1) & 3)) & 3) * 4 + (r >> 3)
                dests[q, at >> 1] = d
                return link[s], at + 1

            _, at = lax.while_loop(more, emit, (head[q * HALF + d], pos))

            @pl.when((at & 1) == 1)
            def _():
                slots[q, at] = 0
                sources[q, at] = HALF

            return at + (at & 1)

        total = lax.fori_loop(0, HALF, segment, 0)

        for i in range(2 * UNROLL):
            slots[q, total + i] = 0
            sources[q, total + i] = HALF
            dests[q, (total >> 1) + (i >> 1)] = 0
        groups[q] = ((total >> 1) + UNROLL - 1) // UNROLL


def make_plan(where, rows, cols, count):
    i32 = jnp.int32
    lists = jax.ShapeDtypeStruct((2, LIST), i32)
    return pl.pallas_call(
        plan_kernel,
        out_shape=(lists, lists, lists, jax.ShapeDtypeStruct((2,), i32)),
        in_specs=[smem()] * 4,
        out_specs=(smem(),) * 4,
        scratch_shapes=[pltpu.SMEM((2 * HALF,), i32), pltpu.SMEM((TILE,), i32)],
        cost_estimate=cost(0, 8),
        name="plan",
    )(where, rows, cols, count)


def turn_kernel(count, v, out):
    def step(i, _):
        for u in range(4):
            out[4 * i + u] = v[0, 0, 4 * i + u].T
        return 0

    lax.fori_loop(0, (count[0, 0] + 3) // 4, step, 0)


def turn_tiles(count, tile_values):
    return pl.pallas_call(
        turn_kernel,
        out_shape=jax.ShapeDtypeStruct(tile_values.shape[2:], tile_values.dtype),
        in_specs=[smem(), vmem()],
        out_specs=vmem(),
        compiler_params=params(),
        cost_estimate=cost(0, 10),
        name="turn",
    )(count, tile_values)


def middle_kernel(got, w, cot, act_out, grad_out, part_out):
    total = got[0].astype(F32)
    for i in range(1, 4):
        total = total + got[i].astype(F32)
    aggregated = total.astype(BF16)
    pre = jnp.dot(aggregated, w[...], preferred_element_type=F32)
    s = jax.nn.sigmoid(pre)
    act_out[...] = (pre * s).astype(BF16)
    grad = (cot[...].astype(F32) * (s * (1.0 + pre * (1.0 - s)))).astype(BF16)
    grad_out[...] = grad
    part = lax.dot_general(aggregated, grad, (((0,), (0,)), ((), ())), preferred_element_type=F32)
    part_out[...] = part.reshape(part_out.shape).astype(BF16)


def middle(got, w, cot):
    n, width = cot.shape
    rows = jax.ShapeDtypeStruct((n, width), BF16)
    return pl.pallas_call(
        middle_kernel,
        out_shape=(rows, rows, jax.ShapeDtypeStruct((ROWS, width // ROWS, width), BF16)),
        compiler_params=params(),
        cost_estimate=cost(4 * n * width * width, 1),
        name="middle",
    )(got, w, cot)


def pack_kernel(grad, parts, out):
    total = parts[0].astype(F32)
    for i in range(1, ROWS):
        total = total + parts[i].astype(F32)
    part = total.astype(BF16)
    for i in range(4):
        out[i, :TILE] = grad[...]
        out[i, TILE:] = part


def pack(grad, parts):
    n, width = grad.shape
    return pl.pallas_call(
        pack_kernel,
        out_shape=jax.ShapeDtypeStruct((4, n + parts.shape[1], width), BF16),
        compiler_params=params(),
        cost_estimate=cost(0, 1),
        name="pack",
    )(grad, parts)


def fold_kernel(got, out):
    total = got[0, TILE:].astype(F32)
    for i in range(1, 4):
        total = total + got[i, TILE:].astype(F32)
    for i in range(4):
        out[TILE * i : TILE * (i + 1)] = got[i, :TILE]
    out[4 * TILE :] = total.astype(BF16)


def fold(got):
    extra, width = got.shape[1] - TILE, got.shape[2]
    return pl.pallas_call(
        fold_kernel,
        out_shape=jax.ShapeDtypeStruct((4 * TILE + extra, width), BF16),
        compiler_params=params(),
        cost_estimate=cost(0, 1),
        name="fold",
    )(got)


def collect_kernel(where, l0, l1, l2, l3, out, slices):
    y = where[1]
    rows = 4 * TILE
    for k, line in enumerate((l0, l1, l2, l3)):
        out[rows * k : rows * (k + 1)] = line[:rows]
        slices[(y - k) & 3] = line[rows:].astype(F32)
    out[4 * rows :] = ((slices[0] + slices[1]) + (slices[2] + slices[3])).astype(BF16)


def collect(where, lines):
    rows, width = lines[0].shape
    extra = rows - 4 * TILE
    return pl.pallas_call(
        collect_kernel,
        out_shape=jax.ShapeDtypeStruct((HALF * TILE + extra, width), BF16),
        in_specs=[smem()] + [vmem()] * 4,
        out_specs=vmem(),
        scratch_shapes=[pltpu.VMEM((4, extra, width), F32)],
        compiler_params=params(),
        cost_estimate=cost(0, 3),
        name="collect",
    )(where, *lines)


def gather_products(q, slots, sources, dests, groups, v, grads, held, acc):
    rows = HALF * TILE
    held[:rows] = grads[:rows]
    held[rows:] = jnp.zeros((TILE, held.shape[1]), BF16)

    def tile(at):
        return held[pl.ds(pl.multiple_of(sources[q, at] * TILE, TILE), TILE)]

    def step(g, _):
        products = []
        for u in range(UNROLL):
            at = (g * UNROLL + u) * 2
            left = jnp.concatenate([v[slots[q, at]], v[slots[q, at + 1]]], axis=1)
            right = jnp.concatenate([tile(at), tile(at + 1)], axis=0)
            products.append(jnp.dot(left, right, preferred_element_type=F32))
        for u in range(UNROLL):
            d = dests[q, g * UNROLL + u]
            acc[d] = acc[d] + products[u]
        return 0

    lax.fori_loop(0, groups[q], step, 0)


def first_kernel(slots, sources, dests, groups, v, grads, acc, held):
    acc[...] = jnp.zeros_like(acc)
    gather_products(0, slots, sources, dests, groups, v, grads, held, acc)


def second_kernel(slots, sources, dests, groups, v, grads, mine, start, out, held, acc):
    acc[...] = start[...]
    gather_products(1, slots, sources, dests, groups, v, grads, held, acc)
    rows = HALF * TILE
    part = (mine[rows:].astype(F32) + grads[rows:].astype(F32)).astype(BF16)
    for d in range(HALF):
        out[d, :TILE] = acc[d].astype(BF16)
        out[d, TILE:] = part


def backward(plan, v, mine, theirs):
    rows, width = mine.shape
    extra = rows - HALF * TILE
    held = pltpu.VMEM(((HALF + 1) * TILE, width), BF16)
    sums = (HALF, TILE, width)
    work = cost(2 * 64 * TILE * TILE * width, 8)
    first = pl.pallas_call(
        first_kernel,
        out_shape=jax.ShapeDtypeStruct(sums, F32),
        in_specs=[smem()] * 4 + [vmem()] * 2,
        out_specs=vmem(),
        scratch_shapes=[held],
        compiler_params=params(),
        cost_estimate=work,
        name="first",
    )(*plan, v, mine)
    return pl.pallas_call(
        second_kernel,
        out_shape=jax.ShapeDtypeStruct((HALF, TILE + extra, width), BF16),
        in_specs=[smem()] * 4 + [vmem()] * 4,
        out_specs=vmem(),
        scratch_shapes=[held, pltpu.VMEM(sums, F32)],
        compiler_params=params(),
        cost_estimate=work,
        name="second",
    )(*plan, v, theirs, mine, first)


def last_kernel(scale, got, w, grad_out, weight_out):
    total = got[0, :TILE].astype(F32)
    for i in range(1, ROWS):
        total = total + got[i, :TILE].astype(F32)
    grad_out[...] = lax.dot_general(
        total.astype(BF16), w[...], (((1,), (1,)), ((), ())), preferred_element_type=F32
    ).astype(BF16)
    extra = got.shape[1] - TILE
    for i in range(ROWS):
        weight_out[extra * i : extra * (i + 1)] = got[i, TILE:].astype(F32) * scale


def last(got, w, scale):
    width = w.shape[0]
    return pl.pallas_call(
        functools.partial(last_kernel, scale),
        out_shape=(
            jax.ShapeDtypeStruct((TILE, width), BF16),
            jax.ShapeDtypeStruct((width, width), F32),
        ),
        compiler_params=params(),
        cost_estimate=cost(2 * TILE * width * width, 1),
        name="last",
    )(got, w)


def shards(features, weight, tile_values, tile_rows, tile_cols, tile_count, cotangent):
    node_dev = features.shape[0]
    grad_scale = 1.0 / math.sqrt(node_dev * lax.axis_size("row") * lax.axis_size("col"))
    c = lax.axis_index("col")
    where = jnp.stack([c >> 3, (c >> 1) & 3, c & 1]).astype(jnp.int32)

    xs = trade_row(jnp.broadcast_to(features[None], (ROWS,) + features.shape))
    give, keep = forward(where, tile_rows, tile_cols, tile_count, tile_values, xs)
    got = send_core(give)
    paired = (keep.astype(F32) + got.astype(F32)).astype(BF16).reshape(4, 4, TILE, -1)
    others = [send_y(paired[k], k).astype(F32) for k in (1, 2, 3)]
    block = (paired[0].astype(F32) + others[0] + others[1] + others[2]).astype(BF16)
    plan = make_plan(where, tile_rows, tile_cols, tile_count)
    turned = turn_tiles(tile_count, tile_values)
    activated, grad_pre, part = middle(trade_zh(block), weight, cotangent)

    line = fold(trade_zh(pack(grad_pre, trade_row(part))))
    mine = collect(where, [line] + [send_y(line, k) for k in (1, 2, 3)])
    spread = backward(plan, turned, mine, send_core(mine))
    grad_features, grad_weight = last(trade_row(spread), weight, grad_scale)
    return (activated, grad_features, grad_weight)


def solution(mesh):
    return jax.shard_map(
        shards,
        mesh=mesh,
        in_specs=(
            P(("col", "row"), None),
            P(),
            P("row", "col", None, None, None),
            P("row", "col", None),
            P("row", "col", None),
            P("row", "col"),
            P(("row", "col"), None),
        ),
        out_specs=(P(("row", "col"), None), P(("col", "row"), None), P()),
        check_vma=False,
    )
```

```python
import functools
import math

import jax
import jax.numpy as jnp
from jax import lax
from jax.experimental import pallas as pl
from jax.experimental.pallas import tpu as pltpu
from jax.sharding import PartitionSpec as P

TILE = 128
SLOTS = 128
ROWS = 16
COLS = 32
HALF = 16
UNROLL = 4
SOURCE = 192
TARGET = 384
LENGTH = 480
PLAN = 512
CHUNK = 16
VMEM_LIMIT = 24 * 1024 * 1024
BF16 = jnp.bfloat16
F32 = jnp.float32


def send_y(v, k):
    pairs = [(c, (c // 8) * 8 + ((c // 2 + k) % 4) * 2 + c % 2) for c in range(COLS)]
    return lax.ppermute(v, "col", pairs)


def send_core(v):
    return lax.ppermute(v, "col", [(c, c ^ 1) for c in range(COLS)])


def trade_row(v):
    return lax.all_to_all(v, "row", 0, 0)


def trade_zh(v):
    groups = [[zh * 8 + rest for zh in range(4)] for rest in range(8)]
    return lax.all_to_all(v, "col", 0, 0, axis_index_groups=groups)


def smem():
    return pl.BlockSpec(memory_space=pltpu.SMEM)


def vmem():
    return pl.BlockSpec(memory_space=pltpu.VMEM)


def params():
    return pltpu.CompilerParams(vmem_limit_bytes=VMEM_LIMIT)


def cost(flops, mib):
    return pl.CostEstimate(flops=flops, bytes_accessed=mib * 1024 * 1024, transcendentals=0)


def plan_kernel(where, rows, cols, count, plan, head, link):
    y, core = where[1], where[2]

    def clear(i, _):
        head[i] = -1
        return 0

    lax.fori_loop(0, 4 * HALF, clear, 0)

    def chain(s, _):
        r, c = rows[0, 0, s], cols[0, 0, s]
        mine = jnp.where((r & 1) == core, HALF, 0)
        forth = mine + ((((r >> 1) & 3) - y) & 3) * 4 + (r >> 3)
        back = 3 * HALF - mine + c
        link[0, s] = head[forth]
        head[forth] = s
        link[1, s] = head[back]
        head[back] = s
        return 0

    lax.fori_loop(0, count[0, 0], chain, 0)

    for q in range(4):
        way = q // 2
        blank = (0, HALF) if way == 0 else (SLOTS, 0)

        def segment(d, pos, q=q, way=way, blank=blank):
            def more(state):
                return state[0] >= 0

            def emit(state):
                s, at = state
                r = rows[0, 0, s]
                plan[q, at] = s
                if way == 0:
                    plan[q, SOURCE + at] = cols[0, 0, s]
                else:
                    plan[q, SOURCE + at] = ((y - ((r >> 1) & 3)) & 3) * 4 + (r >> 3)
                plan[q, TARGET + (at >> 1)] = d
                return link[way, s], at + 1

            _, at = lax.while_loop(more, emit, (head[q * HALF + d], pos))

            @pl.when((at & 1) == 1)
            def _():
                plan[q, at], plan[q, SOURCE + at] = blank

            return at + (at & 1)

        total = lax.fori_loop(0, HALF, segment, 0)

        for i in range(2 * UNROLL):
            plan[q, total + i], plan[q, SOURCE + total + i] = blank
            plan[q, TARGET + (total >> 1) + (i >> 1)] = 0
        plan[q, LENGTH] = ((total >> 1) + UNROLL - 1) // UNROLL


def make_plan(where, rows, cols, count):
    i32 = jnp.int32
    return pl.pallas_call(
        plan_kernel,
        out_shape=jax.ShapeDtypeStruct((4, PLAN), i32),
        in_specs=[smem()] * 4,
        out_specs=smem(),
        scratch_shapes=[pltpu.SMEM((4 * HALF,), i32), pltpu.SMEM((2, SLOTS), i32)],
        cost_estimate=cost(0, 16),
        name="plan",
    )(where, rows, cols, count)


def turn_kernel(count, v, out):
    out[SLOTS] = jnp.zeros((TILE, TILE), BF16)

    def step(i, _):
        for u in range(4):
            out[4 * i + u] = v[0, 0, 4 * i + u].T
        return 0

    lax.fori_loop(0, (count[0, 0] + 3) // 4, step, 0)


def turn_tiles(count, tile_values):
    return pl.pallas_call(
        turn_kernel,
        out_shape=jax.ShapeDtypeStruct((SLOTS + 1, TILE, TILE), BF16),
        in_specs=[smem(), vmem()],
        out_specs=vmem(),
        compiler_params=params(),
        cost_estimate=cost(0, 10),
        name="turn",
    )(count, tile_values)


def middle_kernel(got, w, cot, act_out, grad_out, part_out):
    total = got[0].astype(F32)
    for i in range(1, 4):
        total = total + got[i].astype(F32)
    aggregated = total.astype(BF16)
    pre = jnp.dot(aggregated, w[...], preferred_element_type=F32)
    s = jax.nn.sigmoid(pre)
    act_out[...] = (pre * s).astype(BF16)
    grad = (cot[...].astype(F32) * (s * (1.0 + pre * (1.0 - s)))).astype(BF16)
    grad_out[...] = grad
    part = lax.dot_general(aggregated, grad, (((0,), (0,)), ((), ())), preferred_element_type=F32)
    part_out[...] = part.reshape(part_out.shape).astype(BF16)


def middle(got, w, cot):
    n, width = cot.shape
    rows = jax.ShapeDtypeStruct((n, width), BF16)
    return pl.pallas_call(
        middle_kernel,
        out_shape=(rows, rows, jax.ShapeDtypeStruct((ROWS, width // ROWS, width), BF16)),
        compiler_params=params(),
        cost_estimate=cost(4 * n * width * width, 1),
        name="middle",
    )(got, w, cot)


def pack_kernel(grad, parts, out):
    total = parts[0].astype(F32)
    for i in range(1, ROWS):
        total = total + parts[i].astype(F32)
    part = total.astype(BF16)
    for i in range(4):
        out[i, :TILE] = grad[...]
        out[i, TILE:] = part


def pack(grad, parts):
    n, width = grad.shape
    return pl.pallas_call(
        pack_kernel,
        out_shape=jax.ShapeDtypeStruct((4, n + parts.shape[1], width), BF16),
        compiler_params=params(),
        cost_estimate=cost(0, 1),
        name="pack",
    )(grad, parts)


def fold_kernel(got, out):
    total = got[0, TILE:].astype(F32)
    for i in range(1, 4):
        total = total + got[i, TILE:].astype(F32)
    for i in range(4):
        out[TILE * i : TILE * (i + 1)] = got[i, :TILE]
    out[4 * TILE :] = total.astype(BF16)


def fold(got):
    extra, width = got.shape[1] - TILE, got.shape[2]
    return pl.pallas_call(
        fold_kernel,
        out_shape=jax.ShapeDtypeStruct((4 * TILE + extra, width), BF16),
        compiler_params=params(),
        cost_estimate=cost(0, 1),
        name="fold",
    )(got)


def collect_kernel(where, l0, l1, l2, l3, out, slices):
    y = where[1]
    rows = 4 * TILE
    for k, line in enumerate((l0, l1, l2, l3)):
        out[rows * k : rows * (k + 1)] = line[:rows]
        slices[(y - k) & 3] = line[rows:].astype(F32)
    out[4 * rows :] = ((slices[0] + slices[1]) + (slices[2] + slices[3])).astype(BF16)


def collect(where, lines):
    rows, width = lines[0].shape
    extra = rows - 4 * TILE
    return pl.pallas_call(
        collect_kernel,
        out_shape=jax.ShapeDtypeStruct((HALF * TILE + extra, width), BF16),
        in_specs=[smem()] + [vmem()] * 4,
        out_specs=vmem(),
        scratch_shapes=[pltpu.VMEM((4, extra, width), F32)],
        compiler_params=params(),
        cost_estimate=cost(0, 3),
        name="collect",
    )(where, *lines)


def fetch_tiles(live, v, tiles, sems):
    def chunk(i):
        part = pl.ds(i * CHUNK, CHUNK)
        return pltpu.make_async_copy(v.at[part], tiles.at[part], sems.at[i])

    for i in range(SLOTS // CHUNK):
        pl.when(i * CHUNK < live)(chunk(i).start)

    def arrive():
        for i in range(SLOTS // CHUNK):
            pl.when(i * CHUNK < live)(chunk(i).wait)

    return arrive


def add_products(q, plan, tiles, held, acc):
    def tile(at):
        return held[pl.ds(pl.multiple_of(plan[q, SOURCE + at] * TILE, TILE), TILE)]

    def step(g, _):
        products = []
        for u in range(UNROLL):
            at = (g * UNROLL + u) * 2
            left = jnp.concatenate([tiles[plan[q, at]], tiles[plan[q, at + 1]]], axis=1)
            right = jnp.concatenate([tile(at), tile(at + 1)], axis=0)
            products.append(jnp.dot(left, right, preferred_element_type=F32))
        for u in range(UNROLL):
            d = plan[q, TARGET + g * UNROLL + u]
            acc[d] = acc[d] + products[u]
        return 0

    lax.fori_loop(0, plan[q, LENGTH], step, 0)


def forward_kernel(q, count, plan, v, xs, out, tiles, held, acc, sems):
    arrive = fetch_tiles(count[0, 0], v, tiles, sems)
    held[: HALF * TILE] = xs[...].reshape(HALF * TILE, xs.shape[2])
    held[HALF * TILE :] = jnp.zeros((TILE, xs.shape[2]), BF16)
    acc[...] = jnp.zeros_like(acc)
    arrive()
    add_products(q, plan, tiles, held, acc)
    out[...] = acc[...].astype(BF16)


def forward(q, count, plan, v, xs):
    width = xs.shape[2]
    return pl.pallas_call(
        functools.partial(forward_kernel, q),
        out_shape=jax.ShapeDtypeStruct((HALF, TILE, width), BF16),
        in_specs=[smem()] * 2 + [pl.BlockSpec(memory_space=pltpu.HBM), vmem()],
        out_specs=vmem(),
        scratch_shapes=[
            pltpu.VMEM((SLOTS, TILE, TILE), BF16),
            pltpu.VMEM(((HALF + 1) * TILE, width), BF16),
            pltpu.VMEM((HALF, TILE, width), F32),
            pltpu.SemaphoreType.DMA((SLOTS // CHUNK,)),
        ],
        compiler_params=pltpu.CompilerParams(vmem_limit_bytes=50 * 1024 * 1024),
        cost_estimate=cost(2 * 64 * TILE * TILE * width, 8),
        name="forward",
    )(count, plan, v, xs)


def first_kernel(plan, v, grads, acc):
    acc[...] = jnp.zeros_like(acc)
    add_products(2, plan, v, grads, acc)


def second_kernel(plan, v, grads, mine, start, out, acc):
    acc[...] = start[...]
    add_products(3, plan, v, grads, acc)
    rows = HALF * TILE
    part = (mine[rows:].astype(F32) + grads[rows:].astype(F32)).astype(BF16)
    for d in range(HALF):
        out[d, :TILE] = acc[d].astype(BF16)
        out[d, TILE:] = part


def backward(plan, v, mine, theirs):
    rows, width = mine.shape
    sums = (HALF, TILE, width)
    work = cost(2 * 64 * TILE * TILE * width, 8)
    first = pl.pallas_call(
        first_kernel,
        out_shape=jax.ShapeDtypeStruct(sums, F32),
        in_specs=[smem()] + [vmem()] * 2,
        out_specs=vmem(),
        compiler_params=params(),
        cost_estimate=work,
        name="first",
    )(plan, v, mine)
    return pl.pallas_call(
        second_kernel,
        out_shape=jax.ShapeDtypeStruct((HALF, TILE + rows - HALF * TILE, width), BF16),
        in_specs=[smem()] + [vmem()] * 4,
        out_specs=vmem(),
        scratch_shapes=[pltpu.VMEM(sums, F32)],
        compiler_params=params(),
        cost_estimate=work,
        name="second",
    )(plan, v, theirs, mine, first)


def last_kernel(scale, got, w, grad_out, weight_out):
    total = got[0, :TILE].astype(F32)
    for i in range(1, ROWS):
        total = total + got[i, :TILE].astype(F32)
    grad_out[...] = lax.dot_general(
        total.astype(BF16), w[...], (((1,), (1,)), ((), ())), preferred_element_type=F32
    ).astype(BF16)
    extra = got.shape[1] - TILE
    for i in range(ROWS):
        weight_out[extra * i : extra * (i + 1)] = got[i, TILE:].astype(F32) * scale


def last(got, w, scale):
    width = w.shape[0]
    return pl.pallas_call(
        functools.partial(last_kernel, scale),
        out_shape=(
            jax.ShapeDtypeStruct((TILE, width), BF16),
            jax.ShapeDtypeStruct((width, width), F32),
        ),
        compiler_params=params(),
        cost_estimate=cost(2 * TILE * width * width, 1),
        name="last",
    )(got, w)


def shards(features, weight, tile_values, tile_rows, tile_cols, tile_count, cotangent):
    node_dev = features.shape[0]
    grad_scale = 1.0 / math.sqrt(node_dev * lax.axis_size("row") * lax.axis_size("col"))
    c = lax.axis_index("col")
    where = jnp.stack([c >> 3, (c >> 1) & 3, c & 1]).astype(jnp.int32)

    xs = trade_row(jnp.broadcast_to(features[None], (ROWS,) + features.shape))
    plan = make_plan(where, tile_rows, tile_cols, tile_count)
    turned = turn_tiles(tile_count, tile_values)
    values = tile_values.reshape(tile_values.shape[2:])
    plan, turned, xs = lax.optimization_barrier((plan, turned, xs))

    got = send_core(forward(0, tile_count, plan, values, xs))
    keep = forward(1, tile_count, plan, values, xs)
    paired = (keep.astype(F32) + got.astype(F32)).astype(BF16).reshape(4, 4, TILE, -1)
    others = [send_y(paired[k], k).astype(F32) for k in (1, 2, 3)]
    block = (paired[0].astype(F32) + others[0] + others[1] + others[2]).astype(BF16)
    activated, grad_pre, part = middle(trade_zh(block), weight, cotangent)

    line = fold(trade_zh(pack(grad_pre, trade_row(part))))
    mine = collect(where, [line] + [send_y(line, k) for k in (1, 2, 3)])
    spread = trade_row(backward(plan, turned, mine, send_core(mine)))
    grad_features, grad_weight = last(spread, weight, grad_scale)
    return (activated, grad_features, grad_weight)


def solution(mesh):
    return jax.shard_map(
        shards,
        mesh=mesh,
        in_specs=(
            P(("col", "row"), None),
            P(),
            P("row", "col", None, None, None),
            P("row", "col", None),
            P("row", "col", None),
            P("row", "col"),
            P(("row", "col"), None),
        ),
        out_specs=(P(("row", "col"), None), P(("col", "row"), None), P()),
        check_vma=False,
    )
```

```python
import functools
import math

import jax
import jax.numpy as jnp
from jax import lax
from jax.experimental import pallas as pl
from jax.experimental.pallas import tpu as pltpu
from jax.sharding import PartitionSpec as P

TILE = 128
SLOTS = 128
ROWS = 16
COLS = 32
HALF = 16
UNROLL = 8
SOURCE = 192
TARGET = 384
LENGTH = 480
PLAN = 512
CHUNK = 16
VMEM_LIMIT = 24 * 1024 * 1024
BF16 = jnp.bfloat16
F32 = jnp.float32


def send_y(v, k):
    pairs = [(c, (c // 8) * 8 + ((c // 2 + k) % 4) * 2 + c % 2) for c in range(COLS)]
    return lax.ppermute(v, "col", pairs)


def send_core(v):
    return lax.ppermute(v, "col", [(c, c ^ 1) for c in range(COLS)])


def trade_row(v):
    return lax.all_to_all(v, "row", 0, 0)


def swap_zh(v, k):
    pairs = [(c, ((c // 8) ^ k) * 8 + c % 8) for c in range(COLS)]
    return lax.ppermute(v, "col", pairs)


def trade_near(v):
    groups = [[zh * 8 + rest for rest in range(8)] for zh in range(4)]
    return lax.all_to_all(v, "col", 0, 0, axis_index_groups=groups)


def trade_zh(v):
    groups = [[zh * 8 + rest for zh in range(4)] for rest in range(8)]
    return lax.all_to_all(v, "col", 0, 0, axis_index_groups=groups)


def smem():
    return pl.BlockSpec(memory_space=pltpu.SMEM)


def vmem():
    return pl.BlockSpec(memory_space=pltpu.VMEM)


def params():
    return pltpu.CompilerParams(vmem_limit_bytes=VMEM_LIMIT)


def cost(flops, mib):
    return pl.CostEstimate(flops=flops, bytes_accessed=mib * 1024 * 1024, transcendentals=0)


def plan_kernel(where, rows, cols, count, plan, head, link):
    zh, y, core = where[0], where[1], where[2]

    def clear(i, _):
        head[i] = -1
        return 0

    lax.fori_loop(0, 4 * HALF, clear, 0)

    def chain(s, _):
        r, c = rows[0, 0, s], cols[0, 0, s]
        mine = jnp.where((r & 1) == core, HALF, 0)
        forth = mine + ((((r >> 1) & 3) - y) & 3) * 4 + (r >> 3)
        back = 3 * HALF - mine + c
        link[0, s] = head[forth]
        head[forth] = s
        link[1, s] = head[back]
        head[back] = s
        return 0

    lax.fori_loop(0, count[0, 0], chain, 0)

    for q in range(4):
        way = q // 2
        blank = (0, HALF) if way == 0 else (SLOTS, 0)

        def segment(d, pos, q=q, way=way, blank=blank):
            def more(state):
                return state[0] >= 0

            def emit(state):
                s, at = state
                r = rows[0, 0, s]
                plan[q, at] = s
                if way == 0:
                    plan[q, SOURCE + at] = cols[0, 0, s]
                else:
                    far = (r >> 3) ^ zh
                    near = (y - ((r >> 1) & 3)) & 3
                    plan[q, SOURCE + at] = near * 4 + (far ^ (far >> 1))
                plan[q, TARGET + (at >> 1)] = d
                return link[way, s], at + 1

            _, at = lax.while_loop(more, emit, (head[q * HALF + d], pos))

            @pl.when((at & 1) == 1)
            def _():
                plan[q, at], plan[q, SOURCE + at] = blank

            return at + (at & 1)

        total = lax.fori_loop(0, HALF, segment, 0)

        for i in range(2 * UNROLL):
            plan[q, total + i], plan[q, SOURCE + total + i] = blank
            plan[q, TARGET + (total >> 1) + (i >> 1)] = 0
        plan[q, LENGTH] = ((total >> 1) + UNROLL - 1) // UNROLL


def make_plan(where, rows, cols, count):
    i32 = jnp.int32
    return pl.pallas_call(
        plan_kernel,
        out_shape=jax.ShapeDtypeStruct((4, PLAN), i32),
        in_specs=[smem()] * 4,
        out_specs=smem(),
        scratch_shapes=[pltpu.SMEM((4 * HALF,), i32), pltpu.SMEM((2, SLOTS), i32)],
        cost_estimate=cost(0, 16),
        name="plan",
    )(where, rows, cols, count)


def turn_kernel(count, v, out):
    def step(i, _):
        for u in range(4):
            out[4 * i + u] = v[0, 0, 4 * i + u].T
        return 0

    lax.fori_loop(0, (count[0, 0] + 3) // 4, step, 0)


def turn_tiles(count, tile_values):
    return pl.pallas_call(
        turn_kernel,
        out_shape=jax.ShapeDtypeStruct((SLOTS, TILE, TILE), BF16),
        in_specs=[smem(), vmem()],
        out_specs=vmem(),
        compiler_params=params(),
        cost_estimate=cost(0, 10),
        name="turn",
    )(count, tile_values)


def middle_kernel(got, w, cot, act_out, grad_out, part_out):
    total = got[0].astype(F32)
    for i in range(1, 4):
        total = total + got[i].astype(F32)
    aggregated = total.astype(BF16)
    pre = jnp.dot(aggregated, w[...], preferred_element_type=F32)
    s = jax.nn.sigmoid(pre)
    act_out[...] = (pre * s).astype(BF16)
    grad = (cot[...].astype(F32) * (s * (1.0 + pre * (1.0 - s)))).astype(BF16)
    grad_out[...] = grad
    part = lax.dot_general(aggregated, grad, (((0,), (0,)), ((), ())), preferred_element_type=F32)
    part_out[...] = part.reshape(part_out.shape).astype(BF16)


def middle(got, w, cot):
    n, width = cot.shape
    rows = jax.ShapeDtypeStruct((n, width), BF16)
    return pl.pallas_call(
        middle_kernel,
        out_shape=(rows, rows, jax.ShapeDtypeStruct((ROWS, width // ROWS, width), BF16)),
        compiler_params=params(),
        cost_estimate=cost(4 * n * width * width, 1),
        name="middle",
    )(got, w, cot)


def sum_parts_kernel(parts, out):
    total = parts[0].astype(F32)
    for i in range(1, parts.shape[0]):
        total = total + parts[i].astype(F32)
    part = total.astype(BF16)
    for i in range(out.shape[0]):
        out[i] = part


def sum_parts(parts, copies):
    return pl.pallas_call(
        sum_parts_kernel,
        out_shape=jax.ShapeDtypeStruct((copies,) + parts.shape[1:], BF16),
        compiler_params=params(),
        cost_estimate=cost(0, 1),
        name="sum_parts",
    )(parts)


def fetch_tiles(live, v, tiles, sems):
    def chunk(i):
        part = pl.ds(i * CHUNK, CHUNK)
        return pltpu.make_async_copy(v.at[part], tiles.at[part], sems.at[i])

    for i in range(SLOTS // CHUNK):
        pl.when(i * CHUNK < live)(chunk(i).start)

    def arrive():
        for i in range(SLOTS // CHUNK):
            pl.when(i * CHUNK < live)(chunk(i).wait)

    return arrive


def add_products(q, plan, tiles, held, acc):
    def tile(at):
        return held[pl.ds(pl.multiple_of(plan[q, SOURCE + at] * TILE, TILE), TILE)]

    def step(g, _):
        products = []
        for u in range(UNROLL):
            at = (g * UNROLL + u) * 2
            left = jnp.concatenate([tiles[plan[q, at]], tiles[plan[q, at + 1]]], axis=1)
            right = jnp.concatenate([tile(at), tile(at + 1)], axis=0)
            products.append(jnp.dot(left, right, preferred_element_type=F32))
        for u in range(UNROLL):
            d = plan[q, TARGET + g * UNROLL + u]
            acc[d] = acc[d] + products[u]
        return 0

    lax.fori_loop(0, plan[q, LENGTH], step, 0)


def forward_kernel(q, count, plan, v, xs, out, tiles, sems, held, acc):
    arrive = fetch_tiles(count[0, 0], v, tiles, sems)
    held[: HALF * TILE] = xs[...].reshape(HALF * TILE, xs.shape[2])
    held[HALF * TILE :] = jnp.zeros((TILE, xs.shape[2]), BF16)
    acc[...] = jnp.zeros_like(acc)
    arrive()
    add_products(q, plan, tiles, held, acc)
    out[...] = acc[...].astype(BF16)


def first_kernel(count, plan, v, grads, acc, tiles, sems):
    arrive = fetch_tiles(count[0, 0], v, tiles, sems)
    acc[...] = jnp.zeros_like(acc)
    tiles[SLOTS] = jnp.zeros((TILE, TILE), BF16)
    arrive()
    add_products(2, plan, tiles, grads, acc)


def second_kernel(count, plan, v, grads, parts, start, out, tiles, sems, acc):
    arrive = fetch_tiles(count[0, 0], v, tiles, sems)
    acc[...] = start[...]
    tiles[SLOTS] = jnp.zeros((TILE, TILE), BF16)
    total = parts[0].astype(F32)
    for i in range(1, parts.shape[0]):
        total = total + parts[i].astype(F32)
    part = total.astype(BF16)
    arrive()
    add_products(3, plan, tiles, grads, acc)
    for d in range(HALF):
        out[d, :TILE] = acc[d].astype(BF16)
        out[d, TILE:] = part


def block_product(kernel, name, out, scratch, count, plan, v, *operands):
    return pl.pallas_call(
        kernel,
        out_shape=out,
        in_specs=[smem()] * 2 + [pl.BlockSpec(memory_space=pltpu.HBM)] + [vmem()] * len(operands),
        out_specs=vmem(),
        scratch_shapes=[
            pltpu.VMEM((SLOTS + 1, TILE, TILE), BF16),
            pltpu.SemaphoreType.DMA((SLOTS // CHUNK,)),
            *scratch,
        ],
        compiler_params=pltpu.CompilerParams(vmem_limit_bytes=50 * 1024 * 1024),
        cost_estimate=cost(2 * 64 * TILE * TILE * out.shape[2], 8),
        name=name,
    )(count, plan, v, *operands)


def forward(q, count, plan, v, xs):
    width = xs.shape[2]
    kernel = functools.partial(forward_kernel, q)
    out = jax.ShapeDtypeStruct((HALF, TILE, width), BF16)
    scratch = [pltpu.VMEM(((HALF + 1) * TILE, width), BF16), pltpu.VMEM((HALF, TILE, width), F32)]
    return block_product(kernel, "forward", out, scratch, count, plan, v, xs)


def backward(count, plan, v, mine, theirs, parts):
    width = mine.shape[1]
    sums = (HALF, TILE, width)
    out = jax.ShapeDtypeStruct(sums, F32)
    first = block_product(first_kernel, "first", out, [], count, plan, v, mine)
    out = jax.ShapeDtypeStruct((HALF, TILE + parts.shape[1], width), BF16)
    scratch = [pltpu.VMEM(sums, F32)]
    return block_product(
        second_kernel, "second", out, scratch, count, plan, v, theirs, parts, first
    )


def last_kernel(scale, got, w, grad_out, weight_out):
    total = got[0, :TILE].astype(F32)
    for i in range(1, ROWS):
        total = total + got[i, :TILE].astype(F32)
    grad_out[...] = lax.dot_general(
        total.astype(BF16), w[...], (((1,), (1,)), ((), ())), preferred_element_type=F32
    ).astype(BF16)
    extra = got.shape[1] - TILE
    for i in range(ROWS):
        weight_out[extra * i : extra * (i + 1)] = got[i, TILE:].astype(F32) * scale


def last(got, w, scale):
    width = w.shape[0]
    return pl.pallas_call(
        functools.partial(last_kernel, scale),
        out_shape=(
            jax.ShapeDtypeStruct((TILE, width), BF16),
            jax.ShapeDtypeStruct((width, width), F32),
        ),
        compiler_params=params(),
        cost_estimate=cost(2 * TILE * width * width, 1),
        name="last",
    )(got, w)


def shards(features, weight, tile_values, tile_rows, tile_cols, tile_count, cotangent):
    node_dev = features.shape[0]
    grad_scale = 1.0 / math.sqrt(node_dev * lax.axis_size("row") * lax.axis_size("col"))
    c = lax.axis_index("col")
    where = jnp.stack([c >> 3, (c >> 1) & 3, c & 1]).astype(jnp.int32)

    xs = trade_row(jnp.broadcast_to(features[None], (ROWS,) + features.shape))
    plan = make_plan(where, tile_rows, tile_cols, tile_count)
    turned = turn_tiles(tile_count, tile_values)
    values = tile_values.reshape(tile_values.shape[2:])
    plan, turned, xs = lax.optimization_barrier((plan, turned, xs))

    got = send_core(forward(0, tile_count, plan, values, xs))
    keep = forward(1, tile_count, plan, values, xs)
    paired = (keep.astype(F32) + got.astype(F32)).astype(BF16).reshape(4, 4, TILE, -1)
    others = [send_y(paired[k], k).astype(F32) for k in (1, 2, 3)]
    block = (paired[0].astype(F32) + others[0] + others[1] + others[2]).astype(BF16)
    activated, grad_pre, part = middle(trade_zh(block), weight, cotangent)

    part = sum_parts(trade_row(part), 4)
    pair = jnp.concatenate([grad_pre, swap_zh(grad_pre, 1)], axis=0)
    line = jnp.concatenate([pair, swap_zh(pair, 3)], axis=0)
    line, part = lax.optimization_barrier((line, part))
    part = sum_parts(trade_zh(part), 8)
    mine = jnp.concatenate([line] + [send_y(line, k) for k in (1, 2, 3)], axis=0)
    mine, part = lax.optimization_barrier((mine, part))
    spread = trade_row(backward(tile_count, plan, turned, mine, send_core(mine), trade_near(part)))
    grad_features, grad_weight = last(spread, weight, grad_scale)
    return (activated, grad_features, grad_weight)


def solution(mesh):
    return jax.shard_map(
        shards,
        mesh=mesh,
        in_specs=(
            P(("col", "row"), None),
            P(),
            P("row", "col", None, None, None),
            P("row", "col", None),
            P("row", "col", None),
            P("row", "col"),
            P(("row", "col"), None),
        ),
        out_specs=(P(("row", "col"), None), P(("col", "row"), None), P()),
        check_vma=False,
    )
```

```python
import functools
import math

import jax
import jax.numpy as jnp
from jax import lax
from jax.experimental import pallas as pl
from jax.experimental.pallas import tpu as pltpu
from jax.sharding import PartitionSpec as P

TILE = 128
ROWS = 16
COLS = 32
HALF = 16
GROUP = 8
CHUNK = 16
SLOTS = 128
VMEM_LIMIT = 24 * 1024 * 1024
BF16 = jnp.bfloat16
F32 = jnp.float32


def send_y(v, k):
    pairs = [(c, (c // 8) * 8 + ((c // 2 + k) % 4) * 2 + c % 2) for c in range(COLS)]
    return lax.ppermute(v, "col", pairs)


def send_core(v):
    return lax.ppermute(v, "col", [(c, c ^ 1) for c in range(COLS)])


def trade_row(v):
    return lax.all_to_all(v, "row", 0, 0)


def trade_zh(v):
    groups = [[zh * 8 + rest for zh in range(4)] for rest in range(8)]
    return lax.all_to_all(v, "col", 0, 0, axis_index_groups=groups)


def smem():
    return pl.BlockSpec(memory_space=pltpu.SMEM)


def vmem():
    return pl.BlockSpec(memory_space=pltpu.VMEM)


def params():
    return pltpu.CompilerParams(vmem_limit_bytes=VMEM_LIMIT)


def cost(flops, mib):
    return pl.CostEstimate(flops=flops, bytes_accessed=mib * 1024 * 1024, transcendentals=0)


def choose_slots(parity, where, rows, slots):
    live = where[3]

    def pick(g, found):
        for u in range(GROUP):
            s = g * GROUP + u
            slots[found] = s
            chosen = ((rows[0, 0, s] & 1) == parity) & (s < live)
            found = found + jnp.where(chosen, 1, 0)
        return found

    return lax.fori_loop(0, (live + GROUP - 1) // GROUP, pick, 0)


def add_products(found, slots, tile, source, target, acc):
    def step(g, _):
        products, targets = [], []
        for u in range(GROUP):
            at = g * GROUP + u
            s = jnp.where(at < found, slots[at], 0)
            targets.append(jnp.where(at < found, target(s), HALF))
            products.append(jnp.dot(tile(s), source(s), preferred_element_type=F32))
        for u in range(GROUP):
            acc[targets[u]] = acc[targets[u]] + products[u]
        return 0

    lax.fori_loop(0, (found + GROUP - 1) // GROUP, step, 0)


def fetch_tiles(live, v, tiles, sems):
    def chunk(i):
        part = pl.ds(i * CHUNK, CHUNK)
        return pltpu.make_async_copy(v.at[0, 0, part], tiles.at[part], sems.at[i])

    for i in range(SLOTS // CHUNK):
        pl.when(i * CHUNK < live)(chunk(i).start)

    def arrive():
        for i in range(SLOTS // CHUNK):
            pl.when(i * CHUNK < live)(chunk(i).wait)

    return arrive


def forward_kernel(other, where, rows, cols, v, xs, out, slots, acc, tiles, sems):
    y, core = where[1], where[2]
    arrive = fetch_tiles(where[3], v, tiles, sems)
    acc[...] = jnp.zeros_like(acc)
    found = choose_slots(core ^ other, where, rows, slots)

    def target(s):
        r = rows[0, 0, s]
        return ((((r >> 1) & 3) - y) & 3) * 4 + (r >> 3)

    arrive()
    add_products(found, slots, lambda s: tiles[s], lambda s: xs[cols[0, 0, s]], target, acc)
    out[...] = acc[:HALF].astype(BF16)


def forward(other, where, rows, cols, values, xs):
    width = xs.shape[-1]
    return pl.pallas_call(
        functools.partial(forward_kernel, other),
        out_shape=jax.ShapeDtypeStruct((HALF, TILE, width), BF16),
        in_specs=[smem()] * 3 + [pl.BlockSpec(memory_space=pltpu.HBM), vmem()],
        out_specs=vmem(),
        scratch_shapes=[
            pltpu.SMEM((SLOTS + GROUP,), jnp.int32),
            pltpu.VMEM((HALF + 1, TILE, width), F32),
            pltpu.VMEM((SLOTS, TILE, TILE), BF16),
            pltpu.SemaphoreType.DMA((SLOTS // CHUNK,)),
        ],
        compiler_params=pltpu.CompilerParams(vmem_limit_bytes=50 * 1024 * 1024),
        cost_estimate=cost(2 * 64 * TILE * TILE * width, 7),
        name="forward",
    )(where, rows, cols, values, xs)


def turn_kernel(where, v, out):
    def step(i, _):
        for u in range(4):
            out[4 * i + u] = v[0, 0, 4 * i + u].T
        return 0

    lax.fori_loop(0, (where[3] + 3) // 4, step, 0)


def turn_tiles(where, tile_values):
    return pl.pallas_call(
        turn_kernel,
        out_shape=jax.ShapeDtypeStruct(tile_values.shape[2:], tile_values.dtype),
        in_specs=[smem(), vmem()],
        out_specs=vmem(),
        compiler_params=params(),
        cost_estimate=cost(0, 10),
        name="turn",
    )(where, tile_values)


def middle_kernel(got, w, cot, act_out, grad_out, part_out):
    total = got[0].astype(F32)
    for i in range(1, 4):
        total = total + got[i].astype(F32)
    aggregated = total.astype(BF16)
    pre = jnp.dot(aggregated, w[...], preferred_element_type=F32)
    s = jax.nn.sigmoid(pre)
    act_out[...] = (pre * s).astype(BF16)
    grad = (cot[...].astype(F32) * (s * (1.0 + pre * (1.0 - s)))).astype(BF16)
    grad_out[...] = grad
    part = lax.dot_general(aggregated, grad, (((0,), (0,)), ((), ())), preferred_element_type=F32)
    part_out[...] = part.reshape(part_out.shape).astype(BF16)


def middle(got, w, cot):
    n, width = cot.shape
    rows = jax.ShapeDtypeStruct((n, width), BF16)
    return pl.pallas_call(
        middle_kernel,
        out_shape=(rows, rows, jax.ShapeDtypeStruct((ROWS, width // ROWS, width), BF16)),
        compiler_params=params(),
        cost_estimate=cost(4 * n * width * width, 1),
        name="middle",
    )(got, w, cot)


def pack_kernel(grad, parts, out):
    total = parts[0].astype(F32)
    for i in range(1, ROWS):
        total = total + parts[i].astype(F32)
    part = total.astype(BF16)
    for i in range(4):
        out[i, :TILE] = grad[...]
        out[i, TILE:] = part


def pack(grad, parts):
    n, width = grad.shape
    return pl.pallas_call(
        pack_kernel,
        out_shape=jax.ShapeDtypeStruct((4, n + parts.shape[1], width), BF16),
        compiler_params=params(),
        cost_estimate=cost(0, 1),
        name="pack",
    )(grad, parts)


def fold_kernel(got, out):
    total = got[0, TILE:].astype(F32)
    for i in range(1, 4):
        total = total + got[i, TILE:].astype(F32)
    for i in range(4):
        out[TILE * i : TILE * (i + 1)] = got[i, :TILE]
    out[4 * TILE :] = total.astype(BF16)


def fold(got):
    extra, width = got.shape[1] - TILE, got.shape[2]
    return pl.pallas_call(
        fold_kernel,
        out_shape=jax.ShapeDtypeStruct((4 * TILE + extra, width), BF16),
        compiler_params=params(),
        cost_estimate=cost(0, 1),
        name="fold",
    )(got)


def collect_kernel(where, l0, l1, l2, l3, out, slices):
    y = where[1]
    rows = 4 * TILE
    for k, line in enumerate((l0, l1, l2, l3)):
        out[rows * k : rows * (k + 1)] = line[:rows]
        slices[(y - k) & 3] = line[rows:].astype(F32)
    out[4 * rows :] = ((slices[0] + slices[1]) + (slices[2] + slices[3])).astype(BF16)


def collect(where, lines):
    rows, width = lines[0].shape
    extra = rows - 4 * TILE
    return pl.pallas_call(
        collect_kernel,
        out_shape=jax.ShapeDtypeStruct((HALF * TILE + extra, width), BF16),
        in_specs=[smem()] + [vmem()] * 4,
        out_specs=vmem(),
        scratch_shapes=[pltpu.VMEM((4, extra, width), F32)],
        compiler_params=params(),
        cost_estimate=cost(0, 3),
        name="collect",
    )(where, *lines)


def backward_half(other, where, rows, cols, v, grads, slots, acc):
    y, core = where[1], where[2]
    found = choose_slots(core ^ other, where, rows, slots)

    def source(s):
        r = rows[0, 0, s]
        at = ((y - ((r >> 1) & 3)) & 3) * 4 + (r >> 3)
        return grads[pl.ds(pl.multiple_of(at * TILE, TILE), TILE)]

    add_products(found, slots, lambda s: v[s], source, lambda s: cols[0, 0, s], acc)


def first_kernel(where, rows, cols, v, grads, out, slots, acc):
    acc[...] = jnp.zeros_like(acc)
    backward_half(0, where, rows, cols, v, grads, slots, acc)
    out[...] = acc[:HALF]


def second_kernel(where, rows, cols, v, grads, mine, start, out, slots, acc):
    acc[:HALF] = start[...]
    acc[HALF] = jnp.zeros_like(acc[HALF])
    backward_half(1, where, rows, cols, v, grads, slots, acc)
    rest = HALF * TILE
    part = (mine[rest:].astype(F32) + grads[rest:].astype(F32)).astype(BF16)
    for d in range(HALF):
        out[d, :TILE] = acc[d].astype(BF16)
        out[d, TILE:] = part


def backward(where, rows, cols, v, mine, theirs):
    extra, width = mine.shape[0] - HALF * TILE, mine.shape[1]
    scratch = [
        pltpu.SMEM((SLOTS + GROUP,), jnp.int32),
        pltpu.VMEM((HALF + 1, TILE, width), F32),
    ]
    work = cost(2 * 64 * TILE * TILE * width, 8)
    first = pl.pallas_call(
        first_kernel,
        out_shape=jax.ShapeDtypeStruct((HALF, TILE, width), F32),
        in_specs=[smem()] * 3 + [vmem()] * 2,
        out_specs=vmem(),
        scratch_shapes=scratch,
        compiler_params=params(),
        cost_estimate=work,
        name="first",
    )(where, rows, cols, v, mine)
    return pl.pallas_call(
        second_kernel,
        out_shape=jax.ShapeDtypeStruct((HALF, TILE + extra, width), BF16),
        in_specs=[smem()] * 3 + [vmem()] * 4,
        out_specs=vmem(),
        scratch_shapes=scratch,
        compiler_params=params(),
        cost_estimate=work,
        name="second",
    )(where, rows, cols, v, theirs, mine, first)


def last_kernel(scale, got, w, grad_out, weight_out):
    total = got[0, :TILE].astype(F32)
    for i in range(1, ROWS):
        total = total + got[i, :TILE].astype(F32)
    grad_out[...] = lax.dot_general(
        total.astype(BF16), w[...], (((1,), (1,)), ((), ())), preferred_element_type=F32
    ).astype(BF16)
    extra = got.shape[1] - TILE
    for i in range(ROWS):
        weight_out[extra * i : extra * (i + 1)] = got[i, TILE:].astype(F32) * scale


def last(got, w, scale):
    width = w.shape[0]
    return pl.pallas_call(
        functools.partial(last_kernel, scale),
        out_shape=(
            jax.ShapeDtypeStruct((TILE, width), BF16),
            jax.ShapeDtypeStruct((width, width), F32),
        ),
        compiler_params=params(),
        cost_estimate=cost(2 * TILE * width * width, 1),
        name="last",
    )(got, w)


def shards(features, weight, tile_values, tile_rows, tile_cols, tile_count, cotangent):
    node_dev = features.shape[0]
    grad_scale = 1.0 / math.sqrt(node_dev * lax.axis_size("row") * lax.axis_size("col"))
    c = lax.axis_index("col")
    where = jnp.stack([c >> 3, (c >> 1) & 3, c & 1, tile_count[0, 0]]).astype(jnp.int32)

    features, where = lax.optimization_barrier((features, where))
    xs = trade_row(jnp.broadcast_to(features[None], (ROWS,) + features.shape))
    xs, where = lax.optimization_barrier((xs, where))
    block = (where, tile_rows, tile_cols)
    got = send_core(forward(1, *block, tile_values, xs))
    keep = forward(0, *block, tile_values, xs)
    paired = (keep.astype(F32) + got.astype(F32)).astype(BF16).reshape(4, 4, TILE, -1)
    others = [send_y(paired[k], k).astype(F32) for k in (1, 2, 3)]
    rows = (paired[0].astype(F32) + others[0] + others[1] + others[2]).astype(BF16)
    turned = turn_tiles(where, tile_values)
    rows, turned = lax.optimization_barrier((rows, turned))
    activated, grad_pre, part = middle(trade_zh(rows), weight, cotangent)

    line = fold(trade_zh(pack(grad_pre, trade_row(part))))
    mine = collect(where, [line] + [send_y(line, k) for k in (1, 2, 3)])
    spread = backward(*block, turned, mine, send_core(mine))
    grad_features, grad_weight = last(trade_row(spread), weight, grad_scale)
    return (activated, grad_features, grad_weight)


def solution(mesh):
    return jax.shard_map(
        shards,
        mesh=mesh,
        in_specs=(
            P(("col", "row"), None),
            P(),
            P("row", "col", None, None, None),
            P("row", "col", None),
            P("row", "col", None),
            P("row", "col"),
            P(("row", "col"), None),
        ),
        out_specs=(P(("row", "col"), None), P(("col", "row"), None), P()),
        check_vma=False,
    )
```

```python
import functools
import math

import jax
import jax.numpy as jnp
from jax import lax
from jax.experimental import pallas as pl
from jax.experimental.pallas import tpu as pltpu
from jax.sharding import PartitionSpec as P

TILE = 128
ROWS = 16
COLS = 32
HALF = 16
GROUP = 8
CHUNK = 16
SLOTS = 128
VMEM_LIMIT = 24 * 1024 * 1024
BF16 = jnp.bfloat16
F32 = jnp.float32


def send_y(v, k):
    pairs = [(c, (c // 8) * 8 + ((c // 2 + k) % 4) * 2 + c % 2) for c in range(COLS)]
    return lax.ppermute(v, "col", pairs)


def send_x(v, k):
    pairs = [(r, (r // 4) * 4 + (r + k) % 4) for r in range(ROWS)]
    return lax.ppermute(v, "row", pairs)


def send_core(v):
    return lax.ppermute(v, "col", [(c, c ^ 1) for c in range(COLS)])


def trade_row(v):
    return lax.all_to_all(v, "row", 0, 0)


def trade_zl(v):
    groups = [[zl * 4 + x for zl in range(4)] for x in range(4)]
    return lax.all_to_all(v, "row", 0, 0, axis_index_groups=groups)


def trade_zh(v):
    groups = [[zh * 8 + rest for zh in range(4)] for rest in range(8)]
    return lax.all_to_all(v, "col", 0, 0, axis_index_groups=groups)


def smem():
    return pl.BlockSpec(memory_space=pltpu.SMEM)


def vmem():
    return pl.BlockSpec(memory_space=pltpu.VMEM)


def params():
    return pltpu.CompilerParams(vmem_limit_bytes=VMEM_LIMIT)


def cost(flops, mib):
    return pl.CostEstimate(flops=flops, bytes_accessed=mib * 1024 * 1024, transcendentals=0)


def choose_slots(parity, where, rows, slots):
    live = where[3]

    def pick(g, found):
        for u in range(GROUP):
            s = g * GROUP + u
            slots[found] = s
            chosen = ((rows[0, 0, s] & 1) == parity) & (s < live)
            found = found + jnp.where(chosen, 1, 0)
        return found

    return lax.fori_loop(0, (live + GROUP - 1) // GROUP, pick, 0)


def add_products(found, slots, tile, source, target, acc):
    def step(g, _):
        products, targets = [], []
        for u in range(GROUP):
            at = g * GROUP + u
            s = jnp.where(at < found, slots[at], 0)
            targets.append(jnp.where(at < found, target(s), HALF))
            products.append(jnp.dot(tile(s), source(s), preferred_element_type=F32))
        for u in range(GROUP):
            acc[targets[u]] = acc[targets[u]] + products[u]
        return 0

    lax.fori_loop(0, (found + GROUP - 1) // GROUP, step, 0)


def pair_kernel(a, b, o0, o2, o1, o3):
    for k, out in enumerate((o0, o1, o2, o3)):
        block = slice(4 * k, 4 * (k + 1))
        out[...] = (a[block].astype(F32) + b[block].astype(F32)).astype(BF16)


def pair(a, b):
    block = jax.ShapeDtypeStruct((4,) + a.shape[1:], BF16)
    none, two, one, three = pl.pallas_call(
        pair_kernel,
        out_shape=(block,) * 4,
        compiler_params=params(),
        cost_estimate=cost(0, 4),
        name="pair",
    )(a, b)
    return none, one, two, three


def fetch_tiles(live, v, tiles, sems):
    def chunk(i):
        part = pl.ds(i * CHUNK, CHUNK)
        return pltpu.make_async_copy(v.at[0, 0, part], tiles.at[part], sems.at[i])

    for i in range(SLOTS // CHUNK):
        pl.when(i * CHUNK < live)(chunk(i).start)

    def arrive():
        for i in range(SLOTS // CHUNK):
            pl.when(i * CHUNK < live)(chunk(i).wait)

    return arrive


def forward_kernel(other, where, rows, cols, v, xs, out, slots, acc, tiles, sems):
    y, core = where[1], where[2]
    arrive = fetch_tiles(where[3], v, tiles, sems)
    acc[...] = jnp.zeros_like(acc)
    found = choose_slots(core ^ other, where, rows, slots)

    def target(s):
        r = rows[0, 0, s]
        return ((((r >> 1) & 3) - y) & 3) * 4 + (r >> 3)

    arrive()
    add_products(found, slots, lambda s: tiles[s], lambda s: xs[cols[0, 0, s]], target, acc)
    out[...] = acc[:HALF].astype(BF16)


def forward(other, where, rows, cols, values, xs):
    width = xs.shape[-1]
    return pl.pallas_call(
        functools.partial(forward_kernel, other),
        out_shape=jax.ShapeDtypeStruct((HALF, TILE, width), BF16),
        in_specs=[smem()] * 3 + [pl.BlockSpec(memory_space=pltpu.HBM), vmem()],
        out_specs=vmem(),
        scratch_shapes=[
            pltpu.SMEM((SLOTS + GROUP,), jnp.int32),
            pltpu.VMEM((HALF + 1, TILE, width), F32),
            pltpu.VMEM((SLOTS, TILE, TILE), BF16),
            pltpu.SemaphoreType.DMA((SLOTS // CHUNK,)),
        ],
        compiler_params=pltpu.CompilerParams(vmem_limit_bytes=50 * 1024 * 1024),
        cost_estimate=cost(2 * 64 * TILE * TILE * width, 7),
        name="forward",
    )(where, rows, cols, values, xs)


def turn_kernel(where, v, out):
    def step(i, _):
        for u in range(4):
            out[4 * i + u] = v[0, 0, 4 * i + u].T
        return 0

    lax.fori_loop(0, (where[3] + 3) // 4, step, 0)


def turn_tiles(where, tile_values):
    return pl.pallas_call(
        turn_kernel,
        out_shape=jax.ShapeDtypeStruct(tile_values.shape[2:], tile_values.dtype),
        in_specs=[smem(), vmem()],
        out_specs=vmem(),
        compiler_params=params(),
        cost_estimate=cost(0, 10),
        name="turn",
    )(where, tile_values)


def middle_kernel(got, w, cot, act_out, grad_out, part_out):
    total = got[0].astype(F32)
    for i in range(1, 4):
        total = total + got[i].astype(F32)
    aggregated = total.astype(BF16)
    pre = jnp.dot(aggregated, w[...], preferred_element_type=F32)
    s = jax.nn.sigmoid(pre)
    act_out[...] = (pre * s).astype(BF16)
    grad = (cot[...].astype(F32) * (s * (1.0 + pre * (1.0 - s)))).astype(BF16)
    grad_out[...] = grad
    part = lax.dot_general(aggregated, grad, (((0,), (0,)), ((), ())), preferred_element_type=F32)
    part_out[...] = part.reshape(part_out.shape).astype(BF16)


def middle(got, w, cot):
    n, width = cot.shape
    rows = jax.ShapeDtypeStruct((n, width), BF16)
    return pl.pallas_call(
        middle_kernel,
        out_shape=(rows, rows, jax.ShapeDtypeStruct((ROWS, width // ROWS, width), BF16)),
        compiler_params=params(),
        cost_estimate=cost(4 * n * width * width, 1),
        name="middle",
    )(got, w, cot)


def pack_kernel(grad, parts, out):
    total = parts[0].astype(F32)
    for i in range(1, ROWS):
        total = total + parts[i].astype(F32)
    part = total.astype(BF16)
    for i in range(4):
        out[i, :TILE] = grad[...]
        out[i, TILE:] = part


def pack(grad, parts):
    n, width = grad.shape
    return pl.pallas_call(
        pack_kernel,
        out_shape=jax.ShapeDtypeStruct((4, n + parts.shape[1], width), BF16),
        compiler_params=params(),
        cost_estimate=cost(0, 1),
        name="pack",
    )(grad, parts)


def fold_kernel(got, out):
    total = got[0, TILE:].astype(F32)
    for i in range(1, 4):
        total = total + got[i, TILE:].astype(F32)
    for i in range(4):
        out[TILE * i : TILE * (i + 1)] = got[i, :TILE]
    out[4 * TILE :] = total.astype(BF16)


def fold(got):
    extra, width = got.shape[1] - TILE, got.shape[2]
    return pl.pallas_call(
        fold_kernel,
        out_shape=jax.ShapeDtypeStruct((4 * TILE + extra, width), BF16),
        compiler_params=params(),
        cost_estimate=cost(0, 1),
        name="fold",
    )(got)


def collect_kernel(where, l0, l1, l2, l3, out, slices):
    y = where[1]
    rows = 4 * TILE
    for k, line in enumerate((l0, l1, l2, l3)):
        out[rows * k : rows * (k + 1)] = line[:rows]
        slices[(y - k) & 3] = line[rows:].astype(F32)
    out[4 * rows :] = ((slices[0] + slices[1]) + (slices[2] + slices[3])).astype(BF16)


def collect(where, lines):
    rows, width = lines[0].shape
    extra = rows - 4 * TILE
    return pl.pallas_call(
        collect_kernel,
        out_shape=jax.ShapeDtypeStruct((HALF * TILE + extra, width), BF16),
        in_specs=[smem()] + [vmem()] * 4,
        out_specs=vmem(),
        scratch_shapes=[pltpu.VMEM((4, extra, width), F32)],
        compiler_params=params(),
        cost_estimate=cost(0, 3),
        name="collect",
    )(where, *lines)


def backward_half(other, where, rows, cols, v, grads, slots, acc):
    y, core, x = where[1], where[2], where[4]
    found = choose_slots(core ^ other, where, rows, slots)

    def source(s):
        r = rows[0, 0, s]
        at = ((y - ((r >> 1) & 3)) & 3) * 4 + (r >> 3)
        return grads[pl.ds(pl.multiple_of(at * TILE, TILE), TILE)]

    def target(s):
        c = cols[0, 0, s]
        return (((c & 3) - x) & 3) * 4 + (c >> 2)

    add_products(found, slots, lambda s: v[s], source, target, acc)


def first_kernel(where, rows, cols, v, grads, out, slots, acc):
    acc[...] = jnp.zeros_like(acc)
    backward_half(0, where, rows, cols, v, grads, slots, acc)
    out[...] = acc[:HALF]


def second_kernel(where, rows, cols, v, grads, mine, start, o0, o2, o1, o3, slots, acc):
    acc[:HALF] = start[...]
    acc[HALF] = jnp.zeros_like(acc[HALF])
    backward_half(1, where, rows, cols, v, grads, slots, acc)
    rest = HALF * TILE
    part = (mine[rest:].astype(F32) + grads[rest:].astype(F32)).astype(BF16)
    for k, out in enumerate((o0, o1, o2, o3)):
        for i in range(4):
            out[TILE * i : TILE * (i + 1)] = acc[4 * k + i].astype(BF16)
        out[4 * TILE :] = part


def backward(where, rows, cols, v, mine, theirs):
    extra, width = mine.shape[0] - HALF * TILE, mine.shape[1]
    scratch = [
        pltpu.SMEM((SLOTS + GROUP,), jnp.int32),
        pltpu.VMEM((HALF + 1, TILE, width), F32),
    ]
    work = cost(2 * 64 * TILE * TILE * width, 8)
    first = pl.pallas_call(
        first_kernel,
        out_shape=jax.ShapeDtypeStruct((HALF, TILE, width), F32),
        in_specs=[smem()] * 3 + [vmem()] * 2,
        out_specs=vmem(),
        scratch_shapes=scratch,
        compiler_params=params(),
        cost_estimate=work,
        name="first",
    )(where, rows, cols, v, mine)
    none, two, one, three = pl.pallas_call(
        second_kernel,
        out_shape=(jax.ShapeDtypeStruct((4 * TILE + extra, width), BF16),) * 4,
        in_specs=[smem()] * 3 + [vmem()] * 4,
        out_specs=(vmem(),) * 4,
        scratch_shapes=scratch,
        compiler_params=params(),
        cost_estimate=work,
        name="second",
    )(where, rows, cols, v, theirs, mine, first)
    return none, one, two, three


def merge_kernel(where, p0, p2, p1, p3, out):
    x = where[4]
    parts = (p0, p1, p2, p3)
    extra = p0.shape[0] - 4 * TILE
    for i in range(4):
        block = slice(TILE * i, TILE * (i + 1))
        total = p0[block].astype(F32)
        for part in parts[1:]:
            total = total + part[block].astype(F32)
        out[i, :TILE] = total.astype(BF16)
        for k, part in enumerate(parts):
            at = pl.multiple_of(TILE + ((x - k) & 3) * extra, extra)
            out[i, pl.ds(at, extra)] = part[4 * TILE :]


def merge(where, parts):
    rows, width = parts[0].shape
    return pl.pallas_call(
        merge_kernel,
        out_shape=jax.ShapeDtypeStruct((4, TILE + 4 * (rows - 4 * TILE), width), BF16),
        in_specs=[smem()] + [vmem()] * 4,
        out_specs=vmem(),
        compiler_params=params(),
        cost_estimate=cost(0, 2),
        name="merge",
    )(where, parts[0], parts[2], parts[1], parts[3])


def last_kernel(scale, got, w, grad_out, weight_out):
    total = got[0, :TILE].astype(F32)
    for i in range(1, 4):
        total = total + got[i, :TILE].astype(F32)
    grad_out[...] = lax.dot_general(
        total.astype(BF16), w[...], (((1,), (1,)), ((), ())), preferred_element_type=F32
    ).astype(BF16)
    extra = got.shape[1] - TILE
    for i in range(4):
        weight_out[extra * i : extra * (i + 1)] = got[i, TILE:].astype(F32) * scale


def last(got, w, scale):
    width = w.shape[0]
    return pl.pallas_call(
        functools.partial(last_kernel, scale),
        out_shape=(
            jax.ShapeDtypeStruct((TILE, width), BF16),
            jax.ShapeDtypeStruct((width, width), F32),
        ),
        compiler_params=params(),
        cost_estimate=cost(2 * TILE * width * width, 1),
        name="last",
    )(got, w)


def shards(features, weight, tile_values, tile_rows, tile_cols, tile_count, cotangent):
    node_dev = features.shape[0]
    grad_scale = 1.0 / math.sqrt(node_dev * lax.axis_size("row") * lax.axis_size("col"))
    r, c = lax.axis_index("row"), lax.axis_index("col")
    where = jnp.stack([c >> 3, (c >> 1) & 3, c & 1, tile_count[0, 0], r & 3]).astype(jnp.int32)

    features, where = lax.optimization_barrier((features, where))
    xs = trade_row(jnp.broadcast_to(features[None], (ROWS,) + features.shape))
    xs, where = lax.optimization_barrier((xs, where))
    block = (where, tile_rows, tile_cols)
    got = send_core(forward(1, *block, tile_values, xs))
    keep = forward(0, *block, tile_values, xs)
    paired = pair(keep, got)
    got = [paired[0]] + [send_y(paired[k], k) for k in (2, 1, 3)]
    got = [v.astype(F32) for v in got]
    rows = (got[0] + got[1] + got[2] + got[3]).astype(BF16)
    turned = turn_tiles(where, tile_values)
    rows, turned = lax.optimization_barrier((rows, turned))
    activated, grad_pre, part = middle(trade_zh(rows), weight, cotangent)

    line = fold(trade_zh(pack(grad_pre, trade_row(part))))
    mine = collect(where, [line] + [send_y(line, k) for k in (1, 2, 3)])
    spread = backward(*block, turned, mine, send_core(mine))
    spread = [spread[0]] + [send_x(spread[k], k) for k in (1, 2, 3)]
    grad_features, grad_weight = last(trade_zl(merge(where, spread)), weight, grad_scale)
    return (activated, grad_features, grad_weight)


def solution(mesh):
    return jax.shard_map(
        shards,
        mesh=mesh,
        in_specs=(
            P(("col", "row"), None),
            P(),
            P("row", "col", None, None, None),
            P("row", "col", None),
            P("row", "col", None),
            P("row", "col"),
            P(("row", "col"), None),
        ),
        out_specs=(P(("row", "col"), None), P(("col", "row"), None), P()),
        check_vma=False,
    )
```

```python
import functools
import math

import jax
import jax.numpy as jnp
from jax import lax
from jax.experimental import pallas as pl
from jax.experimental.pallas import tpu as pltpu
from jax.sharding import PartitionSpec as P

TILE = 128
ROWS = 16
COLS = 32
HALF = 16
GROUP = 8
CHUNK = 16
SLOTS = 128
VMEM_LIMIT = 24 * 1024 * 1024
BF16 = jnp.bfloat16
F32 = jnp.float32


def send_y(v, k):
    pairs = [(c, (c // 8) * 8 + ((c // 2 + k) % 4) * 2 + c % 2) for c in range(COLS)]
    return lax.ppermute(v, "col", pairs)


def send_x(v, k):
    pairs = [(r, (r // 4) * 4 + (r + k) % 4) for r in range(ROWS)]
    return lax.ppermute(v, "row", pairs)


def send_core(v):
    return lax.ppermute(v, "col", [(c, c ^ 1) for c in range(COLS)])


def swap_zl(v, k):
    return lax.ppermute(v, "row", [(r, r ^ (4 * k)) for r in range(ROWS)])


def swap_x(v, k):
    return lax.ppermute(v, "row", [(r, r ^ k) for r in range(ROWS)])


def swap_zh(v, k):
    return lax.ppermute(v, "col", [(c, c ^ (8 * k)) for c in range(COLS)])


def halve(part, bit, swap):
    low, high = jnp.split(part, 2, axis=0)
    give = jnp.where(bit == 1, low, high).astype(BF16)
    return jnp.where(bit == 1, high, low) + swap(give).astype(F32)


def exchange(part, swap):
    part = part.astype(BF16)
    return part.astype(F32) + swap(part).astype(F32)


def trade_row(v):
    return lax.all_to_all(v, "row", 0, 0)


def trade_zl(v):
    groups = [[zl * 4 + x for zl in range(4)] for x in range(4)]
    return lax.all_to_all(v, "row", 0, 0, axis_index_groups=groups)


def trade_zh(v):
    groups = [[zh * 8 + rest for zh in range(4)] for rest in range(8)]
    return lax.all_to_all(v, "col", 0, 0, axis_index_groups=groups)


def smem():
    return pl.BlockSpec(memory_space=pltpu.SMEM)


def vmem():
    return pl.BlockSpec(memory_space=pltpu.VMEM)


def params():
    return pltpu.CompilerParams(vmem_limit_bytes=VMEM_LIMIT)


def cost(flops, mib):
    return pl.CostEstimate(flops=flops, bytes_accessed=mib * 1024 * 1024, transcendentals=0)


def choose_slots(parity, where, rows, slots):
    live = where[3]

    def pick(g, found):
        for u in range(GROUP):
            s = g * GROUP + u
            slots[found] = s
            chosen = ((rows[0, 0, s] & 1) == parity) & (s < live)
            found = found + jnp.where(chosen, 1, 0)
        return found

    return lax.fori_loop(0, (live + GROUP - 1) // GROUP, pick, 0)


def add_products(found, slots, tile, source, target, acc):
    def step(g, _):
        products, targets = [], []
        for u in range(GROUP):
            at = g * GROUP + u
            s = jnp.where(at < found, slots[at], 0)
            targets.append(jnp.where(at < found, target(s), HALF))
            products.append(jnp.dot(tile(s), source(s), preferred_element_type=F32))
        for u in range(GROUP):
            acc[targets[u]] = acc[targets[u]] + products[u]
        return 0

    lax.fori_loop(0, (found + GROUP - 1) // GROUP, step, 0)


def pair_kernel(a, b, o0, o2, o1, o3):
    for k, out in enumerate((o0, o1, o2, o3)):
        block = slice(4 * k, 4 * (k + 1))
        out[...] = (a[block].astype(F32) + b[block].astype(F32)).astype(BF16)


def pair(a, b):
    block = jax.ShapeDtypeStruct((4,) + a.shape[1:], BF16)
    none, two, one, three = pl.pallas_call(
        pair_kernel,
        out_shape=(block,) * 4,
        compiler_params=params(),
        cost_estimate=cost(0, 4),
        name="pair",
    )(a, b)
    return none, one, two, three


def fetch_tiles(live, v, tiles, sems):
    def chunk(i):
        part = pl.ds(i * CHUNK, CHUNK)
        return pltpu.make_async_copy(v.at[part], tiles.at[part], sems.at[i])

    for i in range(SLOTS // CHUNK):
        pl.when(i * CHUNK < live)(chunk(i).start)

    def arrive():
        for i in range(SLOTS // CHUNK):
            pl.when(i * CHUNK < live)(chunk(i).wait)

    return arrive


def forward_kernel(other, where, rows, cols, v, xs, out, slots, acc, tiles, sems):
    y, core = where[1], where[2]
    arrive = fetch_tiles(where[3], v, tiles, sems)
    acc[...] = jnp.zeros_like(acc)
    found = choose_slots(core ^ other, where, rows, slots)

    def target(s):
        r = rows[0, 0, s]
        return ((((r >> 1) & 3) - y) & 3) * 4 + (r >> 3)

    arrive()
    add_products(found, slots, lambda s: tiles[s], lambda s: xs[cols[0, 0, s]], target, acc)
    out[...] = acc[:HALF].astype(BF16)


def forward(other, where, rows, cols, values, xs):
    kernel = functools.partial(forward_kernel, other)
    out = jax.ShapeDtypeStruct((HALF, TILE, xs.shape[-1]), BF16)
    return block_product(kernel, "forward", out, where, rows, cols, values, xs)


def turn_kernel(where, v, out):
    def step(i, _):
        for u in range(4):
            out[4 * i + u] = v[0, 0, 4 * i + u].T
        return 0

    lax.fori_loop(0, (where[3] + 3) // 4, step, 0)


def turn_tiles(where, tile_values):
    return pl.pallas_call(
        turn_kernel,
        out_shape=jax.ShapeDtypeStruct(tile_values.shape[2:], tile_values.dtype),
        in_specs=[smem(), vmem()],
        out_specs=vmem(),
        compiler_params=params(),
        cost_estimate=cost(0, 10),
        name="turn",
    )(where, tile_values)


def middle_kernel(got, w, cot, act_out, grad_out, part_out):
    total = got[0].astype(F32)
    for i in range(1, 4):
        total = total + got[i].astype(F32)
    aggregated = total.astype(BF16)
    pre = jnp.dot(aggregated, w[...], preferred_element_type=F32)
    s = jax.nn.sigmoid(pre)
    act_out[...] = (pre * s).astype(BF16)
    grad = (cot[...].astype(F32) * (s * (1.0 + pre * (1.0 - s)))).astype(BF16)
    grad_out[...] = grad
    part_out[...] = lax.dot_general(
        aggregated, grad, (((0,), (0,)), ((), ())), preferred_element_type=F32
    )


def middle(got, w, cot):
    n, width = cot.shape
    rows = jax.ShapeDtypeStruct((n, width), BF16)
    return pl.pallas_call(
        middle_kernel,
        out_shape=(rows, rows, jax.ShapeDtypeStruct((width, width), F32)),
        compiler_params=params(),
        cost_estimate=cost(4 * n * width * width, 1),
        name="middle",
    )(got, w, cot)


def collect_kernel(where, l0, l1, l2, l3, out, slices):
    y = where[1]
    rows = 4 * TILE
    for k, line in enumerate((l0, l1, l2, l3)):
        out[rows * k : rows * (k + 1)] = line[:rows]
        slices[(y - k) & 3] = line[rows:].astype(F32)
    out[4 * rows :] = ((slices[0] + slices[1]) + (slices[2] + slices[3])).astype(BF16)


def collect(where, lines):
    rows, width = lines[0].shape
    extra = rows - 4 * TILE
    return pl.pallas_call(
        collect_kernel,
        out_shape=jax.ShapeDtypeStruct((HALF * TILE + extra, width), BF16),
        in_specs=[smem()] + [vmem()] * 4,
        out_specs=vmem(),
        scratch_shapes=[pltpu.VMEM((4, extra, width), F32)],
        compiler_params=params(),
        cost_estimate=cost(0, 3),
        name="collect",
    )(where, *lines)


def backward_half(other, where, rows, cols, grads, slots, acc, tiles, arrive):
    y, core, x = where[1], where[2], where[4]
    found = choose_slots(core ^ other, where, rows, slots)

    def source(s):
        r = rows[0, 0, s]
        at = ((y - ((r >> 1) & 3)) & 3) * 4 + (r >> 3)
        return grads[pl.ds(pl.multiple_of(at * TILE, TILE), TILE)]

    def target(s):
        c = cols[0, 0, s]
        return (((c & 3) - x) & 3) * 4 + (c >> 2)

    arrive()
    add_products(found, slots, lambda s: tiles[s], source, target, acc)


def first_kernel(where, rows, cols, v, grads, out, slots, acc, tiles, sems):
    arrive = fetch_tiles(where[3], v, tiles, sems)
    acc[...] = jnp.zeros_like(acc)
    backward_half(0, where, rows, cols, grads, slots, acc, tiles, arrive)
    out[...] = acc[:HALF]


def second_kernel(
    where, rows, cols, v, grads, mine, start, o0, o2, o1, o3, part, slots, acc, tiles, sems
):
    arrive = fetch_tiles(where[3], v, tiles, sems)
    acc[:HALF] = start[...]
    acc[HALF] = jnp.zeros_like(acc[HALF])
    backward_half(1, where, rows, cols, grads, slots, acc, tiles, arrive)
    for k, out in enumerate((o0, o1, o2, o3)):
        for i in range(4):
            out[TILE * i : TILE * (i + 1)] = acc[4 * k + i].astype(BF16)
    rest = HALF * TILE
    part[...] = (mine[rest:].astype(F32) + grads[rest:].astype(F32)).astype(BF16)


def block_product(kernel, name, out, where, rows, cols, v, *operands):
    width = operands[0].shape[-1]
    return pl.pallas_call(
        kernel,
        out_shape=out,
        in_specs=[smem()] * 3 + [pl.BlockSpec(memory_space=pltpu.HBM)] + [vmem()] * len(operands),
        out_specs=jax.tree.map(lambda _: vmem(), out),
        scratch_shapes=[
            pltpu.SMEM((SLOTS + GROUP,), jnp.int32),
            pltpu.VMEM((HALF + 1, TILE, width), F32),
            pltpu.VMEM((SLOTS, TILE, TILE), BF16),
            pltpu.SemaphoreType.DMA((SLOTS // CHUNK,)),
        ],
        compiler_params=pltpu.CompilerParams(vmem_limit_bytes=50 * 1024 * 1024),
        cost_estimate=cost(2 * 64 * TILE * TILE * width, 8),
        name=name,
    )(where, rows, cols, v, *operands)


def backward(where, rows, cols, v, mine, theirs):
    extra, width = mine.shape[0] - HALF * TILE, mine.shape[1]
    out = jax.ShapeDtypeStruct((HALF, TILE, width), F32)
    first = block_product(first_kernel, "first", out, where, rows, cols, v, mine)
    block = jax.ShapeDtypeStruct((4 * TILE, width), BF16)
    out = (block,) * 4 + (jax.ShapeDtypeStruct((extra, width), BF16),)
    none, two, one, three, part = block_product(
        second_kernel, "second", out, where, rows, cols, v, theirs, mine, first
    )
    return (none, one, two, three), part


def merge_kernel(p0, p2, p1, p3, part, out):
    for i in range(4):
        block = slice(TILE * i, TILE * (i + 1))
        total = p0[block].astype(F32)
        for other in (p1, p2, p3):
            total = total + other[block].astype(F32)
        out[i, :TILE] = total.astype(BF16)
        out[i, TILE:] = part[...].astype(BF16)


def merge(parts, part):
    width = part.shape[1]
    return pl.pallas_call(
        merge_kernel,
        out_shape=jax.ShapeDtypeStruct((4, TILE + part.shape[0], width), BF16),
        compiler_params=params(),
        cost_estimate=cost(0, 2),
        name="merge",
    )(parts[0], parts[2], parts[1], parts[3], part)


def last_kernel(scale, got, w, grad_out, weight_out):
    total = got[0, :TILE].astype(F32)
    for i in range(1, 4):
        total = total + got[i, :TILE].astype(F32)
    grad_out[...] = lax.dot_general(
        total.astype(BF16), w[...], (((1,), (1,)), ((), ())), preferred_element_type=F32
    ).astype(BF16)
    extra = got.shape[1] - TILE
    for i in range(4):
        weight_out[extra * i : extra * (i + 1)] = got[i, TILE:].astype(F32) * scale


def last(got, w, scale):
    width = w.shape[0]
    return pl.pallas_call(
        functools.partial(last_kernel, scale),
        out_shape=(
            jax.ShapeDtypeStruct((TILE, width), BF16),
            jax.ShapeDtypeStruct((width, width), F32),
        ),
        compiler_params=params(),
        cost_estimate=cost(2 * TILE * width * width, 1),
        name="last",
    )(got, w)


def shards(features, weight, tile_values, tile_rows, tile_cols, tile_count, cotangent):
    node_dev = features.shape[0]
    grad_scale = 1.0 / math.sqrt(node_dev * lax.axis_size("row") * lax.axis_size("col"))
    r, c = lax.axis_index("row"), lax.axis_index("col")
    where = jnp.stack([c >> 3, (c >> 1) & 3, c & 1, tile_count[0, 0], r & 3]).astype(jnp.int32)

    features, where = lax.optimization_barrier((features, where))
    xs = trade_row(jnp.broadcast_to(features[None], (ROWS,) + features.shape))
    xs, where = lax.optimization_barrier((xs, where))
    block = (where, tile_rows, tile_cols)
    values = tile_values.reshape(tile_values.shape[2:])
    got = send_core(forward(1, *block, values, xs))
    keep = forward(0, *block, values, xs)
    paired = pair(keep, got)
    got = [paired[0]] + [send_y(paired[k], k) for k in (2, 1, 3)]
    got = [v.astype(F32) for v in got]
    rows = (got[0] + got[1] + got[2] + got[3]).astype(BF16)
    turned = turn_tiles(where, tile_values)
    rows, turned = lax.optimization_barrier((rows, turned))
    activated, grad_pre, part = middle(trade_zh(rows), weight, cotangent)

    line = trade_zh(jnp.broadcast_to(grad_pre[None], (4,) + grad_pre.shape))
    line = line.reshape(4 * TILE, -1)
    part = halve(part, r >> 3, lambda v: swap_zl(v, 2))
    part = halve(part, (r >> 2) & 1, lambda v: swap_zl(v, 1))
    part = exchange(part, lambda v: swap_x(v, 1))
    part = exchange(part, lambda v: swap_x(v, 3))
    line = jnp.concatenate([line, part.astype(BF16)], axis=0)
    mine = collect(where, [line] + [send_y(line, k) for k in (1, 2, 3)])
    spread, part = backward(*block, turned, mine, send_core(mine))
    spread = [spread[0]] + [send_x(spread[k], k) for k in (1, 2, 3)]
    part = exchange(part, lambda v: swap_zh(v, 1))
    part = exchange(part, lambda v: swap_zh(v, 3))
    grad_features, grad_weight = last(trade_zl(merge(spread, part)), weight, grad_scale)
    return (activated, grad_features, grad_weight)


def solution(mesh):
    return jax.shard_map(
        shards,
        mesh=mesh,
        in_specs=(
            P(("col", "row"), None),
            P(),
            P("row", "col", None, None, None),
            P("row", "col", None),
            P("row", "col", None),
            P("row", "col"),
            P(("row", "col"), None),
        ),
        out_specs=(P(("row", "col"), None), P(("col", "row"), None), P()),
        check_vma=False,
    )
```

```python
import functools
import math

import jax
import jax.numpy as jnp
from jax import lax
from jax.experimental import pallas as pl
from jax.experimental.pallas import tpu as pltpu
from jax.sharding import PartitionSpec as P

TILE = 128
ROWS = 16
COLS = 32
HALF = 16
GROUP = 16
CHUNK = 16
SLOTS = 128
VMEM_LIMIT = 24 * 1024 * 1024
BF16 = jnp.bfloat16
F32 = jnp.float32


def send_y(v, k):
    pairs = [(c, (c // 8) * 8 + ((c // 2 + k) % 4) * 2 + c % 2) for c in range(COLS)]
    return lax.ppermute(v, "col", pairs)


def send_x(v, k):
    pairs = [(r, (r // 4) * 4 + (r + k) % 4) for r in range(ROWS)]
    return lax.ppermute(v, "row", pairs)


def send_core(v):
    return lax.ppermute(v, "col", [(c, c ^ 1) for c in range(COLS)])


def trade_row(v):
    return lax.all_to_all(v, "row", 0, 0)


def trade_zl(v):
    groups = [[zl * 4 + x for zl in range(4)] for x in range(4)]
    return lax.all_to_all(v, "row", 0, 0, axis_index_groups=groups)


def trade_zh(v):
    groups = [[zh * 8 + rest for zh in range(4)] for rest in range(8)]
    return lax.all_to_all(v, "col", 0, 0, axis_index_groups=groups)


def smem():
    return pl.BlockSpec(memory_space=pltpu.SMEM)


def vmem():
    return pl.BlockSpec(memory_space=pltpu.VMEM)


def params():
    return pltpu.CompilerParams(vmem_limit_bytes=VMEM_LIMIT)


def cost(flops, mib):
    return pl.CostEstimate(flops=flops, bytes_accessed=mib * 1024 * 1024, transcendentals=0)


def choose_slots(parity, where, rows, slots, first, found):
    for u in range(CHUNK):
        s = first + u
        slots[found] = s
        chosen = ((rows[0, 0, s] & 1) == parity) & (s < where[3])
        found = found + jnp.where(chosen, 1, 0)
    return found


def add_products(parity, where, rows, slots, arrive, tile, source, target, acc):
    def group(found, first):
        products, targets = [], []
        for u in range(GROUP):
            at = first + u
            s = jnp.where(at < found, slots[at], 0)
            targets.append(jnp.where(at < found, target(s), HALF))
            products.append(jnp.dot(tile(s), source(s), preferred_element_type=F32))
        for u in range(GROUP):
            acc[targets[u]] = acc[targets[u]] + products[u]

    def chunk(i, state):
        found, done = state
        arrive(i)
        found = choose_slots(parity, where, rows, slots, i * CHUNK, found)
        full = (found - done) >= GROUP
        pl.when(full)(lambda: group(found, done))
        return found, jnp.where(full, done + GROUP, done)

    chunks = (where[3] + CHUNK - 1) // CHUNK
    found, done = lax.fori_loop(0, chunks, chunk, (jnp.int32(0), jnp.int32(0)))
    pl.when(done < found)(lambda: group(found, done))


def pair_kernel(a, b, o0, o2, o1, o3):
    for k, out in enumerate((o0, o1, o2, o3)):
        block = slice(4 * k, 4 * (k + 1))
        out[...] = (a[block].astype(F32) + b[block].astype(F32)).astype(BF16)


def pair(a, b):
    block = jax.ShapeDtypeStruct((4,) + a.shape[1:], BF16)
    none, two, one, three = pl.pallas_call(
        pair_kernel,
        out_shape=(block,) * 4,
        compiler_params=params(),
        cost_estimate=cost(0, 4),
        name="pair",
    )(a, b)
    return none, one, two, three


def fetch_chunks(live, v, tiles, sems):
    def chunk(i):
        part = pl.ds(i * CHUNK, CHUNK)
        return pltpu.make_async_copy(v.at[0, 0, part], tiles.at[part], sems.at[i])

    for i in range(SLOTS // CHUNK):
        pl.when(i * CHUNK < live)(chunk(i).start)
    return chunk


def forward_kernel(other, where, rows, cols, v, xs, out, slots, acc, tiles, sems):
    y, core = where[1], where[2]
    chunks = fetch_chunks(where[3], v, tiles, sems)
    acc[...] = jnp.zeros_like(acc)

    def target(s):
        r = rows[0, 0, s]
        return ((((r >> 1) & 3) - y) & 3) * 4 + (r >> 3)

    add_products(
        core ^ other,
        where,
        rows,
        slots,
        lambda i: chunks(i).wait(),
        lambda s: tiles[s],
        lambda s: xs[cols[0, 0, s]],
        target,
        acc,
    )
    out[...] = acc[:HALF].astype(BF16)


def list_and_sums(width):
    return [
        pltpu.SMEM((SLOTS + GROUP,), jnp.int32),
        pltpu.VMEM((HALF + 1, TILE, width), F32),
    ]


def forward(other, where, rows, cols, values, xs):
    width = xs.shape[-1]
    return pl.pallas_call(
        functools.partial(forward_kernel, other),
        out_shape=jax.ShapeDtypeStruct((HALF, TILE, width), BF16),
        in_specs=[smem()] * 3 + [pl.BlockSpec(memory_space=pltpu.HBM), vmem()],
        out_specs=vmem(),
        scratch_shapes=[
            *list_and_sums(width),
            pltpu.VMEM((SLOTS, TILE, TILE), BF16),
            pltpu.SemaphoreType.DMA((SLOTS // CHUNK,)),
        ],
        compiler_params=pltpu.CompilerParams(vmem_limit_bytes=50 * 1024 * 1024),
        cost_estimate=cost(2 * 64 * TILE * TILE * width, 7),
        name="forward",
    )(where, rows, cols, values, xs)


def turn_kernel(where, v, out, tiles, sems):
    chunks = fetch_chunks(where[3], v, tiles, sems)

    def step(i, _):
        chunks(i).wait()
        for u in range(CHUNK):
            out[i * CHUNK + u] = tiles[i * CHUNK + u].T
        return 0

    lax.fori_loop(0, (where[3] + CHUNK - 1) // CHUNK, step, 0)


def turn_tiles(where, v):
    shape = v.shape[2:]
    return pl.pallas_call(
        turn_kernel,
        out_shape=jax.ShapeDtypeStruct(shape, v.dtype),
        in_specs=[smem(), pl.BlockSpec(memory_space=pltpu.HBM)],
        out_specs=vmem(),
        scratch_shapes=[
            pltpu.VMEM(shape, v.dtype),
            pltpu.SemaphoreType.DMA((SLOTS // CHUNK,)),
        ],
        compiler_params=pltpu.CompilerParams(vmem_limit_bytes=46 * 1024 * 1024),
        cost_estimate=cost(0, 10),
        name="turn",
    )(where, v)


def middle_kernel(got, w, cot, act_out, grad_out, part_out):
    total = got[0].astype(F32)
    for i in range(1, 4):
        total = total + got[i].astype(F32)
    aggregated = total.astype(BF16)
    pre = jnp.dot(aggregated, w[...], preferred_element_type=F32)
    s = jax.nn.sigmoid(pre)
    act_out[...] = (pre * s).astype(BF16)
    grad = (cot[...].astype(F32) * (s * (1.0 + pre * (1.0 - s)))).astype(BF16)
    grad_out[...] = grad
    part = lax.dot_general(aggregated, grad, (((0,), (0,)), ((), ())), preferred_element_type=F32)
    part_out[...] = part.reshape(part_out.shape).astype(BF16)


def middle(got, w, cot):
    n, width = cot.shape
    rows = jax.ShapeDtypeStruct((n, width), BF16)
    return pl.pallas_call(
        middle_kernel,
        out_shape=(rows, rows, jax.ShapeDtypeStruct((ROWS, width // ROWS, width), BF16)),
        compiler_params=params(),
        cost_estimate=cost(4 * n * width * width, 1),
        name="middle",
    )(got, w, cot)


def pack_kernel(grad, parts, out):
    total = parts[0].astype(F32)
    for i in range(1, ROWS):
        total = total + parts[i].astype(F32)
    part = total.astype(BF16)
    for i in range(4):
        out[i, :TILE] = grad[...]
        out[i, TILE:] = part


def pack(grad, parts):
    n, width = grad.shape
    return pl.pallas_call(
        pack_kernel,
        out_shape=jax.ShapeDtypeStruct((4, n + parts.shape[1], width), BF16),
        compiler_params=params(),
        cost_estimate=cost(0, 1),
        name="pack",
    )(grad, parts)


def fold_kernel(got, out):
    total = got[0, TILE:].astype(F32)
    for i in range(1, 4):
        total = total + got[i, TILE:].astype(F32)
    for i in range(4):
        out[TILE * i : TILE * (i + 1)] = got[i, :TILE]
    out[4 * TILE :] = total.astype(BF16)


def fold(got):
    extra, width = got.shape[1] - TILE, got.shape[2]
    return pl.pallas_call(
        fold_kernel,
        out_shape=jax.ShapeDtypeStruct((4 * TILE + extra, width), BF16),
        compiler_params=params(),
        cost_estimate=cost(0, 1),
        name="fold",
    )(got)


def collect_kernel(where, l0, l1, l2, l3, out, slices):
    y = where[1]
    rows = 4 * TILE
    for k, line in enumerate((l0, l1, l2, l3)):
        out[rows * k : rows * (k + 1)] = line[:rows]
        slices[(y - k) & 3] = line[rows:].astype(F32)
    out[4 * rows :] = ((slices[0] + slices[1]) + (slices[2] + slices[3])).astype(BF16)


def collect(where, lines):
    rows, width = lines[0].shape
    extra = rows - 4 * TILE
    return pl.pallas_call(
        collect_kernel,
        out_shape=jax.ShapeDtypeStruct((HALF * TILE + extra, width), BF16),
        in_specs=[smem()] + [vmem()] * 4,
        out_specs=vmem(),
        scratch_shapes=[pltpu.VMEM((4, extra, width), F32)],
        compiler_params=params(),
        cost_estimate=cost(0, 3),
        name="collect",
    )(where, *lines)


def backward_half(other, where, rows, cols, v, grads, slots, acc):
    y, core, x = where[1], where[2], where[4]

    def source(s):
        r = rows[0, 0, s]
        at = ((y - ((r >> 1) & 3)) & 3) * 4 + (r >> 3)
        return grads[pl.ds(pl.multiple_of(at * TILE, TILE), TILE)]

    def target(s):
        c = cols[0, 0, s]
        return (((c & 3) - x) & 3) * 4 + (c >> 2)

    add_products(
        core ^ other, where, rows, slots, lambda i: None, lambda s: v[s], source, target, acc
    )


def first_kernel(where, rows, cols, v, grads, out, slots, acc):
    acc[...] = jnp.zeros_like(acc)
    backward_half(0, where, rows, cols, v, grads, slots, acc)
    out[...] = acc[:HALF]


def second_kernel(where, rows, cols, v, grads, mine, start, o0, o2, o1, o3, slots, acc):
    acc[:HALF] = start[...]
    acc[HALF] = jnp.zeros_like(acc[HALF])
    backward_half(1, where, rows, cols, v, grads, slots, acc)
    rest = HALF * TILE
    part = (mine[rest:].astype(F32) + grads[rest:].astype(F32)).astype(BF16)
    for k, out in enumerate((o0, o1, o2, o3)):
        for i in range(4):
            out[TILE * i : TILE * (i + 1)] = acc[4 * k + i].astype(BF16)
        out[4 * TILE :] = part


def backward(where, rows, cols, v, mine, theirs):
    extra, width = mine.shape[0] - HALF * TILE, mine.shape[1]
    scratch = list_and_sums(width)
    work = cost(2 * 64 * TILE * TILE * width, 8)
    first = pl.pallas_call(
        first_kernel,
        out_shape=jax.ShapeDtypeStruct((HALF, TILE, width), F32),
        in_specs=[smem()] * 3 + [vmem()] * 2,
        out_specs=vmem(),
        scratch_shapes=scratch,
        compiler_params=params(),
        cost_estimate=work,
        name="first",
    )(where, rows, cols, v, mine)
    none, two, one, three = pl.pallas_call(
        second_kernel,
        out_shape=(jax.ShapeDtypeStruct((4 * TILE + extra, width), BF16),) * 4,
        in_specs=[smem()] * 3 + [vmem()] * 4,
        out_specs=(vmem(),) * 4,
        scratch_shapes=scratch,
        compiler_params=params(),
        cost_estimate=work,
        name="second",
    )(where, rows, cols, v, theirs, mine, first)
    return none, one, two, three


def merge_kernel(where, p0, p2, p1, p3, out):
    x = where[4]
    parts = (p0, p1, p2, p3)
    extra = p0.shape[0] - 4 * TILE
    for i in range(4):
        block = slice(TILE * i, TILE * (i + 1))
        total = p0[block].astype(F32)
        for part in parts[1:]:
            total = total + part[block].astype(F32)
        out[i, :TILE] = total.astype(BF16)
        for k, part in enumerate(parts):
            at = pl.multiple_of(TILE + ((x - k) & 3) * extra, extra)
            out[i, pl.ds(at, extra)] = part[4 * TILE :]


def merge(where, parts):
    rows, width = parts[0].shape
    return pl.pallas_call(
        merge_kernel,
        out_shape=jax.ShapeDtypeStruct((4, TILE + 4 * (rows - 4 * TILE), width), BF16),
        in_specs=[smem()] + [vmem()] * 4,
        out_specs=vmem(),
        compiler_params=params(),
        cost_estimate=cost(0, 2),
        name="merge",
    )(where, parts[0], parts[2], parts[1], parts[3])


def last_kernel(scale, got, w, grad_out, weight_out):
    total = got[0, :TILE].astype(F32)
    for i in range(1, 4):
        total = total + got[i, :TILE].astype(F32)
    grad_out[...] = lax.dot_general(
        total.astype(BF16), w[...], (((1,), (1,)), ((), ())), preferred_element_type=F32
    ).astype(BF16)
    extra = got.shape[1] - TILE
    for i in range(4):
        weight_out[extra * i : extra * (i + 1)] = got[i, TILE:].astype(F32) * scale


def last(got, w, scale):
    width = w.shape[0]
    return pl.pallas_call(
        functools.partial(last_kernel, scale),
        out_shape=(
            jax.ShapeDtypeStruct((TILE, width), BF16),
            jax.ShapeDtypeStruct((width, width), F32),
        ),
        compiler_params=params(),
        cost_estimate=cost(2 * TILE * width * width, 1),
        name="last",
    )(got, w)


def shards(features, weight, tile_values, tile_rows, tile_cols, tile_count, cotangent):
    node_dev = features.shape[0]
    grad_scale = 1.0 / math.sqrt(node_dev * lax.axis_size("row") * lax.axis_size("col"))
    r, c = lax.axis_index("row"), lax.axis_index("col")
    where = jnp.stack([c >> 3, (c >> 1) & 3, c & 1, tile_count[0, 0], r & 3]).astype(jnp.int32)

    features, where = lax.optimization_barrier((features, where))
    xs = trade_row(jnp.broadcast_to(features[None], (ROWS,) + features.shape))
    xs, where = lax.optimization_barrier((xs, where))
    block = (where, tile_rows, tile_cols)
    got = send_core(forward(1, *block, tile_values, xs))
    keep = forward(0, *block, tile_values, xs)
    paired = pair(keep, got)
    got = [paired[0]] + [send_y(paired[k], k) for k in (2, 1, 3)]
    got = [v.astype(F32) for v in got]
    rows = (got[0] + got[1] + got[2] + got[3]).astype(BF16)
    turned = turn_tiles(where, tile_values)
    rows, turned = lax.optimization_barrier((rows, turned))
    activated, grad_pre, part = middle(trade_zh(rows), weight, cotangent)

    line = fold(trade_zh(pack(grad_pre, trade_row(part))))
    mine = collect(where, [line] + [send_y(line, k) for k in (1, 2, 3)])
    spread = backward(*block, turned, mine, send_core(mine))
    spread = [spread[0]] + [send_x(spread[k], k) for k in (1, 2, 3)]
    grad_features, grad_weight = last(trade_zl(merge(where, spread)), weight, grad_scale)
    return (activated, grad_features, grad_weight)


def solution(mesh):
    return jax.shard_map(
        shards,
        mesh=mesh,
        in_specs=(
            P(("col", "row"), None),
            P(),
            P("row", "col", None, None, None),
            P("row", "col", None),
            P("row", "col", None),
            P("row", "col"),
            P(("row", "col"), None),
        ),
        out_specs=(P(("row", "col"), None), P(("col", "row"), None), P()),
        check_vma=False,
    )
```

```python
import functools
import math

import jax
import jax.numpy as jnp
from jax import lax
from jax.experimental import pallas as pl
from jax.experimental.pallas import tpu as pltpu
from jax.sharding import PartitionSpec as P

TILE = 128
ROWS = 16
COLS = 32
HALF = 16
GROUP = 16
CHUNK = 16
SLOTS = 128
VMEM_LIMIT = 24 * 1024 * 1024
BF16 = jnp.bfloat16
F32 = jnp.float32


def send_y(v, k):
    pairs = [(c, (c // 8) * 8 + ((c // 2 + k) % 4) * 2 + c % 2) for c in range(COLS)]
    return lax.ppermute(v, "col", pairs)


def send_x(v, k):
    pairs = [(r, (r // 4) * 4 + (r + k) % 4) for r in range(ROWS)]
    return lax.ppermute(v, "row", pairs)


def send_core(v):
    return lax.ppermute(v, "col", [(c, c ^ 1) for c in range(COLS)])


def trade_row(v):
    return lax.all_to_all(v, "row", 0, 0)


def send_zl(v, k):
    return lax.ppermute(v, "row", [(r, (r + 4 * k) % ROWS) for r in range(ROWS)])


def trade_zh(v):
    groups = [[zh * 8 + rest for zh in range(4)] for rest in range(8)]
    return lax.all_to_all(v, "col", 0, 0, axis_index_groups=groups)


def smem():
    return pl.BlockSpec(memory_space=pltpu.SMEM)


def vmem():
    return pl.BlockSpec(memory_space=pltpu.VMEM)


def params():
    return pltpu.CompilerParams(vmem_limit_bytes=VMEM_LIMIT)


def cost(flops, mib):
    return pl.CostEstimate(flops=flops, bytes_accessed=mib * 1024 * 1024, transcendentals=0)


def choose_slots(parity, where, rows, slots, first, found):
    for u in range(CHUNK):
        s = first + u
        slots[found] = s
        chosen = ((rows[0, 0, s] & 1) == parity) & (s < where[3])
        found = found + jnp.where(chosen, 1, 0)
    return found


def add_products(parity, where, rows, slots, arrive, tile, source, target, acc):
    def group(found, first):
        products, targets = [], []
        for u in range(GROUP):
            at = first + u
            s = jnp.where(at < found, slots[at], 0)
            targets.append(jnp.where(at < found, target(s), HALF))
            products.append(jnp.dot(tile(s), source(s), preferred_element_type=F32))
        for u in range(GROUP):
            acc[targets[u]] = acc[targets[u]] + products[u]

    def chunk(i, state):
        found, done = state
        arrive(i)
        found = choose_slots(parity, where, rows, slots, i * CHUNK, found)
        full = (found - done) >= GROUP
        pl.when(full)(lambda: group(found, done))
        return found, jnp.where(full, done + GROUP, done)

    chunks = (where[3] + CHUNK - 1) // CHUNK
    found, done = lax.fori_loop(0, chunks, chunk, (jnp.int32(0), jnp.int32(0)))
    pl.when(done < found)(lambda: group(found, done))


def pair_kernel(a, b, o0, o2, o1, o3):
    for k, out in enumerate((o0, o1, o2, o3)):
        block = slice(4 * k, 4 * (k + 1))
        out[...] = (a[block].astype(F32) + b[block].astype(F32)).astype(BF16)


def pair(a, b):
    block = jax.ShapeDtypeStruct((4,) + a.shape[1:], BF16)
    none, two, one, three = pl.pallas_call(
        pair_kernel,
        out_shape=(block,) * 4,
        compiler_params=params(),
        cost_estimate=cost(0, 4),
        name="pair",
    )(a, b)
    return none, one, two, three


def fetch_chunks(live, v, tiles, sems):
    def chunk(i):
        part = pl.ds(i * CHUNK, CHUNK)
        return pltpu.make_async_copy(v.at[0, 0, part], tiles.at[part], sems.at[i])

    for i in range(SLOTS // CHUNK):
        pl.when(i * CHUNK < live)(chunk(i).start)
    return chunk


def forward_kernel(other, where, rows, cols, v, xs, out, slots, acc, tiles, sems):
    y, core = where[1], where[2]
    chunks = fetch_chunks(where[3], v, tiles, sems)
    acc[...] = jnp.zeros_like(acc)

    def target(s):
        r = rows[0, 0, s]
        return ((((r >> 1) & 3) - y) & 3) * 4 + (r >> 3)

    add_products(
        core ^ other,
        where,
        rows,
        slots,
        lambda i: chunks(i).wait(),
        lambda s: tiles[s],
        lambda s: xs[cols[0, 0, s]],
        target,
        acc,
    )
    out[...] = acc[:HALF].astype(BF16)


def list_and_sums(width):
    return [
        pltpu.SMEM((SLOTS + GROUP,), jnp.int32),
        pltpu.VMEM((HALF + 1, TILE, width), F32),
    ]


def forward(other, where, rows, cols, values, xs):
    width = xs.shape[-1]
    return pl.pallas_call(
        functools.partial(forward_kernel, other),
        out_shape=jax.ShapeDtypeStruct((HALF, TILE, width), BF16),
        in_specs=[smem()] * 3 + [pl.BlockSpec(memory_space=pltpu.HBM), vmem()],
        out_specs=vmem(),
        scratch_shapes=[
            *list_and_sums(width),
            pltpu.VMEM((SLOTS, TILE, TILE), BF16),
            pltpu.SemaphoreType.DMA((SLOTS // CHUNK,)),
        ],
        compiler_params=pltpu.CompilerParams(vmem_limit_bytes=50 * 1024 * 1024),
        cost_estimate=cost(2 * 64 * TILE * TILE * width, 7),
        name="forward",
    )(where, rows, cols, values, xs)


def turn_kernel(where, v, out, tiles, sems):
    chunks = fetch_chunks(where[3], v, tiles, sems)

    def step(i, _):
        chunks(i).wait()
        for u in range(CHUNK):
            out[i * CHUNK + u] = tiles[i * CHUNK + u].T
        return 0

    lax.fori_loop(0, (where[3] + CHUNK - 1) // CHUNK, step, 0)


def turn_tiles(where, v):
    shape = v.shape[2:]
    return pl.pallas_call(
        turn_kernel,
        out_shape=jax.ShapeDtypeStruct(shape, v.dtype),
        in_specs=[smem(), pl.BlockSpec(memory_space=pltpu.HBM)],
        out_specs=vmem(),
        scratch_shapes=[
            pltpu.VMEM(shape, v.dtype),
            pltpu.SemaphoreType.DMA((SLOTS // CHUNK,)),
        ],
        compiler_params=pltpu.CompilerParams(vmem_limit_bytes=46 * 1024 * 1024),
        cost_estimate=cost(0, 10),
        name="turn",
    )(where, v)


def middle_kernel(got, w, cot, act_out, grad_out, part_out):
    total = got[0].astype(F32)
    for i in range(1, 4):
        total = total + got[i].astype(F32)
    aggregated = total.astype(BF16)
    pre = jnp.dot(aggregated, w[...], preferred_element_type=F32)
    s = jax.nn.sigmoid(pre)
    act_out[...] = (pre * s).astype(BF16)
    grad = (cot[...].astype(F32) * (s * (1.0 + pre * (1.0 - s)))).astype(BF16)
    grad_out[...] = grad
    part = lax.dot_general(aggregated, grad, (((0,), (0,)), ((), ())), preferred_element_type=F32)
    part_out[...] = part.reshape(part_out.shape).astype(BF16)


def middle(got, w, cot):
    n, width = cot.shape
    rows = jax.ShapeDtypeStruct((n, width), BF16)
    return pl.pallas_call(
        middle_kernel,
        out_shape=(rows, rows, jax.ShapeDtypeStruct((ROWS, width // ROWS, width), BF16)),
        compiler_params=params(),
        cost_estimate=cost(4 * n * width * width, 1),
        name="middle",
    )(got, w, cot)


def pack_kernel(grad, parts, out):
    total = parts[0].astype(F32)
    for i in range(1, ROWS):
        total = total + parts[i].astype(F32)
    part = total.astype(BF16)
    for i in range(4):
        out[i, :TILE] = grad[...]
        out[i, TILE:] = part


def pack(grad, parts):
    n, width = grad.shape
    return pl.pallas_call(
        pack_kernel,
        out_shape=jax.ShapeDtypeStruct((4, n + parts.shape[1], width), BF16),
        compiler_params=params(),
        cost_estimate=cost(0, 1),
        name="pack",
    )(grad, parts)


def fold_kernel(got, out):
    total = got[0, TILE:].astype(F32)
    for i in range(1, 4):
        total = total + got[i, TILE:].astype(F32)
    for i in range(4):
        out[TILE * i : TILE * (i + 1)] = got[i, :TILE]
    out[4 * TILE :] = total.astype(BF16)


def fold(got):
    extra, width = got.shape[1] - TILE, got.shape[2]
    return pl.pallas_call(
        fold_kernel,
        out_shape=jax.ShapeDtypeStruct((4 * TILE + extra, width), BF16),
        compiler_params=params(),
        cost_estimate=cost(0, 1),
        name="fold",
    )(got)


def collect_kernel(where, l0, l1, l2, l3, out, slices):
    y = where[1]
    rows = 4 * TILE
    for k, line in enumerate((l0, l1, l2, l3)):
        out[rows * k : rows * (k + 1)] = line[:rows]
        slices[(y - k) & 3] = line[rows:].astype(F32)
    out[4 * rows :] = ((slices[0] + slices[1]) + (slices[2] + slices[3])).astype(BF16)


def collect(where, lines):
    rows, width = lines[0].shape
    extra = rows - 4 * TILE
    return pl.pallas_call(
        collect_kernel,
        out_shape=jax.ShapeDtypeStruct((HALF * TILE + extra, width), BF16),
        in_specs=[smem()] + [vmem()] * 4,
        out_specs=vmem(),
        scratch_shapes=[pltpu.VMEM((4, extra, width), F32)],
        compiler_params=params(),
        cost_estimate=cost(0, 3),
        name="collect",
    )(where, *lines)


def backward_half(other, where, rows, cols, v, grads, slots, acc):
    y, core, x = where[1], where[2], where[4]

    def source(s):
        r = rows[0, 0, s]
        at = ((y - ((r >> 1) & 3)) & 3) * 4 + (r >> 3)
        return grads[pl.ds(pl.multiple_of(at * TILE, TILE), TILE)]

    def target(s):
        c = cols[0, 0, s]
        return (((c & 3) - x) & 3) * 4 + (c >> 2)

    add_products(
        core ^ other, where, rows, slots, lambda i: None, lambda s: v[s], source, target, acc
    )


def first_kernel(where, rows, cols, v, grads, out, slots, acc):
    acc[...] = jnp.zeros_like(acc)
    backward_half(0, where, rows, cols, v, grads, slots, acc)
    out[...] = acc[:HALF]


def second_kernel(where, rows, cols, v, grads, mine, start, o0, o2, o1, o3, slots, acc):
    acc[:HALF] = start[...]
    acc[HALF] = jnp.zeros_like(acc[HALF])
    backward_half(1, where, rows, cols, v, grads, slots, acc)
    rest = HALF * TILE
    part = (mine[rest:].astype(F32) + grads[rest:].astype(F32)).astype(BF16)
    for k, out in enumerate((o0, o1, o2, o3)):
        for i in range(4):
            out[TILE * i : TILE * (i + 1)] = acc[4 * k + i].astype(BF16)
        out[4 * TILE :] = part


def backward(where, rows, cols, v, mine, theirs):
    extra, width = mine.shape[0] - HALF * TILE, mine.shape[1]
    scratch = list_and_sums(width)
    work = cost(2 * 64 * TILE * TILE * width, 8)
    first = pl.pallas_call(
        first_kernel,
        out_shape=jax.ShapeDtypeStruct((HALF, TILE, width), F32),
        in_specs=[smem()] * 3 + [vmem()] * 2,
        out_specs=vmem(),
        scratch_shapes=scratch,
        compiler_params=params(),
        cost_estimate=work,
        name="first",
    )(where, rows, cols, v, mine)
    none, two, one, three = pl.pallas_call(
        second_kernel,
        out_shape=(jax.ShapeDtypeStruct((4 * TILE + extra, width), BF16),) * 4,
        in_specs=[smem()] * 3 + [vmem()] * 4,
        out_specs=(vmem(),) * 4,
        scratch_shapes=scratch,
        compiler_params=params(),
        cost_estimate=work,
        name="second",
    )(where, rows, cols, v, theirs, mine, first)
    return none, one, two, three


def merge_kernel(where, p0, p2, p1, p3, o0, o2, o1, o3):
    x, zl = where[4], where[5]
    parts = (p0, p1, p2, p3)
    extra = p0.shape[0] - 4 * TILE
    for i, out in enumerate((o0, o1, o2, o3)):
        block = pl.ds(pl.multiple_of(((zl + i) & 3) * TILE, TILE), TILE)
        total = p0[block].astype(F32)
        for part in parts[1:]:
            total = total + part[block].astype(F32)
        out[:TILE] = total.astype(BF16)
        for k, part in enumerate(parts):
            at = pl.multiple_of(TILE + ((x - k) & 3) * extra, extra)
            out[pl.ds(at, extra)] = part[4 * TILE :]


def merge(where, parts):
    rows, width = parts[0].shape
    block = jax.ShapeDtypeStruct((TILE + 4 * (rows - 4 * TILE), width), BF16)
    none, two, one, three = pl.pallas_call(
        merge_kernel,
        out_shape=(block,) * 4,
        in_specs=[smem()] + [vmem()] * 4,
        out_specs=(vmem(),) * 4,
        compiler_params=params(),
        cost_estimate=cost(0, 2),
        name="merge",
    )(where, parts[0], parts[2], parts[1], parts[3])
    return none, one, two, three


def last_kernel(scale, where, p0, p2, p1, p3, w, grad_out, weight_out):
    zl = where[5]
    parts = (p0, p1, p2, p3)
    total = p0[:TILE].astype(F32)
    for part in parts[1:]:
        total = total + part[:TILE].astype(F32)
    grad_out[...] = lax.dot_general(
        total.astype(BF16), w[...], (((1,), (1,)), ((), ())), preferred_element_type=F32
    ).astype(BF16)
    extra = p0.shape[0] - TILE
    for k, part in enumerate(parts):
        at = pl.multiple_of(((zl - k) & 3) * extra, extra)
        weight_out[pl.ds(at, extra)] = part[TILE:].astype(F32) * scale


def last(where, parts, w, scale):
    width = w.shape[0]
    return pl.pallas_call(
        functools.partial(last_kernel, scale),
        out_shape=(
            jax.ShapeDtypeStruct((TILE, width), BF16),
            jax.ShapeDtypeStruct((width, width), F32),
        ),
        in_specs=[smem()] + [vmem()] * 5,
        out_specs=(vmem(), vmem()),
        compiler_params=params(),
        cost_estimate=cost(2 * TILE * width * width, 1),
        name="last",
    )(where, parts[0], parts[2], parts[1], parts[3], w)


def shards(features, weight, tile_values, tile_rows, tile_cols, tile_count, cotangent):
    node_dev = features.shape[0]
    grad_scale = 1.0 / math.sqrt(node_dev * lax.axis_size("row") * lax.axis_size("col"))
    r, c = lax.axis_index("row"), lax.axis_index("col")
    where = jnp.stack([c >> 3, (c >> 1) & 3, c & 1, tile_count[0, 0], r & 3, r >> 2]).astype(jnp.int32)

    features, where = lax.optimization_barrier((features, where))
    xs = trade_row(jnp.broadcast_to(features[None], (ROWS,) + features.shape))
    xs, where = lax.optimization_barrier((xs, where))
    block = (where, tile_rows, tile_cols)
    got = send_core(forward(1, *block, tile_values, xs))
    keep = forward(0, *block, tile_values, xs)
    paired = pair(keep, got)
    got = [paired[0]] + [send_y(paired[k], k) for k in (2, 1, 3)]
    got = [v.astype(F32) for v in got]
    rows = (got[0] + got[1] + got[2] + got[3]).astype(BF16)
    turned = turn_tiles(where, tile_values)
    rows, turned = lax.optimization_barrier((rows, turned))
    activated, grad_pre, part = middle(trade_zh(rows), weight, cotangent)

    line = fold(trade_zh(pack(grad_pre, trade_row(part))))
    mine = collect(where, [line] + [send_y(line, k) for k in (1, 2, 3)])
    spread = backward(*block, turned, mine, send_core(mine))
    spread = [spread[0]] + [send_x(spread[k], k) for k in (1, 2, 3)]
    pieces = merge(where, spread)
    pieces = [pieces[0]] + [send_zl(pieces[k], k) for k in (1, 2, 3)]
    grad_features, grad_weight = last(where, pieces, weight, grad_scale)
    return (activated, grad_features, grad_weight)


def solution(mesh):
    return jax.shard_map(
        shards,
        mesh=mesh,
        in_specs=(
            P(("col", "row"), None),
            P(),
            P("row", "col", None, None, None),
            P("row", "col", None),
            P("row", "col", None),
            P("row", "col"),
            P(("row", "col"), None),
        ),
        out_specs=(P(("row", "col"), None), P(("col", "row"), None), P()),
        check_vma=False,
    )
```

```python
import functools
import math

import jax
import jax.numpy as jnp
from jax import lax
from jax.experimental import pallas as pl
from jax.experimental.pallas import tpu as pltpu
from jax.sharding import PartitionSpec as P

TILE = 128
ROWS = 16
COLS = 32
HALF = 16
GROUP = 16
CHUNK = 16
SLOTS = 128
VMEM_LIMIT = 24 * 1024 * 1024
BF16 = jnp.bfloat16
F32 = jnp.float32


FIRST, SECOND, TWO = 0, 1, 2


def distance(which, core):
    return 2 if which == TWO else 1 + 2 * (core ^ which)


def send_y(v, which):
    pairs = []
    for c in range(COLS):
        zh, y, core = c // 8, (c // 2) % 4, c % 2
        pairs.append((c, zh * 8 + (y + distance(which, core)) % 4 * 2 + core))
    return lax.ppermute(v, "col", pairs)


def send_x(v, which):
    pairs = []
    for r in range(ROWS):
        for c in range(COLS):
            to = r // 4 * 4 + (r + distance(which, c % 2)) % 4
            pairs.append((r * COLS + c, to * COLS + c))
    return lax.ppermute(v, ("row", "col"), pairs)


def send_core(v):
    return lax.ppermute(v, "col", [(c, c ^ 1) for c in range(COLS)])


def trade_row(v):
    return lax.all_to_all(v, "row", 0, 0)


def trade_zl(v):
    groups = [[zl * 4 + x for zl in range(4)] for x in range(4)]
    return lax.all_to_all(v, "row", 0, 0, axis_index_groups=groups)


def trade_zh(v):
    groups = [[zh * 8 + rest for zh in range(4)] for rest in range(8)]
    return lax.all_to_all(v, "col", 0, 0, axis_index_groups=groups)


def smem():
    return pl.BlockSpec(memory_space=pltpu.SMEM)


def vmem():
    return pl.BlockSpec(memory_space=pltpu.VMEM)


def params():
    return pltpu.CompilerParams(vmem_limit_bytes=VMEM_LIMIT)


def cost(flops, mib):
    return pl.CostEstimate(flops=flops, bytes_accessed=mib * 1024 * 1024, transcendentals=0)


def choose_slots(parity, where, rows, slots, first, found):
    for u in range(CHUNK):
        s = first + u
        slots[found] = s
        chosen = ((rows[0, 0, s] & 1) == parity) & (s < where[3])
        found = found + jnp.where(chosen, 1, 0)
    return found


def add_products(parity, where, rows, slots, arrive, tile, source, target, acc):
    def group(found, first):
        products, targets = [], []
        for u in range(GROUP):
            at = first + u
            s = jnp.where(at < found, slots[at], 0)
            targets.append(jnp.where(at < found, target(s), HALF))
            products.append(jnp.dot(tile(s), source(s), preferred_element_type=F32))
        for u in range(GROUP):
            acc[targets[u]] = acc[targets[u]] + products[u]

    def chunk(i, state):
        found, done = state
        arrive(i)
        found = choose_slots(parity, where, rows, slots, i * CHUNK, found)
        full = (found - done) >= GROUP
        pl.when(full)(lambda: group(found, done))
        return found, jnp.where(full, done + GROUP, done)

    chunks = (where[3] + CHUNK - 1) // CHUNK
    found, done = lax.fori_loop(0, chunks, chunk, (jnp.int32(0), jnp.int32(0)))
    pl.when(done < found)(lambda: group(found, done))


def distances(core):
    return (0, 2, 1 + 2 * core, 3 - 2 * core)


def pair_kernel(where, a, b, *outs):
    for k, out in zip(distances(where[2]), outs):
        span = pl.ds(4 * k, 4)
        out[...] = (a[span].astype(F32) + b[span].astype(F32)).astype(BF16)


def pair(where, a, b):
    block = jax.ShapeDtypeStruct((4,) + a.shape[1:], BF16)
    return pl.pallas_call(
        pair_kernel,
        out_shape=(block,) * 4,
        in_specs=[smem()] + [vmem()] * 2,
        out_specs=(vmem(),) * 4,
        compiler_params=params(),
        cost_estimate=cost(0, 4),
        name="pair",
    )(where, a, b)


def fetch_chunks(live, v, tiles, sems):
    def chunk(i):
        part = pl.ds(i * CHUNK, CHUNK)
        return pltpu.make_async_copy(v.at[0, 0, part], tiles.at[part], sems.at[i])

    for i in range(SLOTS // CHUNK):
        pl.when(i * CHUNK < live)(chunk(i).start)
    return chunk


def forward_kernel(other, where, rows, cols, v, xs, out, slots, acc, tiles, sems):
    y, core = where[1], where[2]
    chunks = fetch_chunks(where[3], v, tiles, sems)
    acc[...] = jnp.zeros_like(acc)

    def target(s):
        r = rows[0, 0, s]
        return ((((r >> 1) & 3) - y) & 3) * 4 + (r >> 3)

    add_products(
        core ^ other,
        where,
        rows,
        slots,
        lambda i: chunks(i).wait(),
        lambda s: tiles[s],
        lambda s: xs[cols[0, 0, s]],
        target,
        acc,
    )
    out[...] = acc[:HALF].astype(BF16)


def list_and_sums(width):
    return [
        pltpu.SMEM((SLOTS + GROUP,), jnp.int32),
        pltpu.VMEM((HALF + 1, TILE, width), F32),
    ]


def forward(other, where, rows, cols, values, xs):
    width = xs.shape[-1]
    return pl.pallas_call(
        functools.partial(forward_kernel, other),
        out_shape=jax.ShapeDtypeStruct((HALF, TILE, width), BF16),
        in_specs=[smem()] * 3 + [pl.BlockSpec(memory_space=pltpu.HBM), vmem()],
        out_specs=vmem(),
        scratch_shapes=[
            *list_and_sums(width),
            pltpu.VMEM((SLOTS, TILE, TILE), BF16),
            pltpu.SemaphoreType.DMA((SLOTS // CHUNK,)),
        ],
        compiler_params=pltpu.CompilerParams(vmem_limit_bytes=50 * 1024 * 1024),
        cost_estimate=cost(2 * 64 * TILE * TILE * width, 7),
        name="forward",
    )(where, rows, cols, values, xs)


def turn_kernel(where, v, out, tiles, sems):
    chunks = fetch_chunks(where[3], v, tiles, sems)

    def step(i, _):
        chunks(i).wait()
        for u in range(CHUNK):
            out[i * CHUNK + u] = tiles[i * CHUNK + u].T
        return 0

    lax.fori_loop(0, (where[3] + CHUNK - 1) // CHUNK, step, 0)


def turn_tiles(where, v):
    shape = v.shape[2:]
    return pl.pallas_call(
        turn_kernel,
        out_shape=jax.ShapeDtypeStruct(shape, v.dtype),
        in_specs=[smem(), pl.BlockSpec(memory_space=pltpu.HBM)],
        out_specs=vmem(),
        scratch_shapes=[
            pltpu.VMEM(shape, v.dtype),
            pltpu.SemaphoreType.DMA((SLOTS // CHUNK,)),
        ],
        compiler_params=pltpu.CompilerParams(vmem_limit_bytes=46 * 1024 * 1024),
        cost_estimate=cost(0, 10),
        name="turn",
    )(where, v)


def middle_kernel(got, w, cot, act_out, grad_out, part_out):
    total = got[0].astype(F32)
    for i in range(1, 4):
        total = total + got[i].astype(F32)
    aggregated = total.astype(BF16)
    pre = jnp.dot(aggregated, w[...], preferred_element_type=F32)
    s = jax.nn.sigmoid(pre)
    act_out[...] = (pre * s).astype(BF16)
    grad = (cot[...].astype(F32) * (s * (1.0 + pre * (1.0 - s)))).astype(BF16)
    grad_out[...] = grad
    part = lax.dot_general(aggregated, grad, (((0,), (0,)), ((), ())), preferred_element_type=F32)
    part_out[...] = part.reshape(part_out.shape).astype(BF16)


def middle(got, w, cot):
    n, width = cot.shape
    rows = jax.ShapeDtypeStruct((n, width), BF16)
    return pl.pallas_call(
        middle_kernel,
        out_shape=(rows, rows, jax.ShapeDtypeStruct((ROWS, width // ROWS, width), BF16)),
        compiler_params=params(),
        cost_estimate=cost(4 * n * width * width, 1),
        name="middle",
    )(got, w, cot)


def pack_kernel(grad, parts, out):
    total = parts[0].astype(F32)
    for i in range(1, ROWS):
        total = total + parts[i].astype(F32)
    part = total.astype(BF16)
    for i in range(4):
        out[i, :TILE] = grad[...]
        out[i, TILE:] = part


def pack(grad, parts):
    n, width = grad.shape
    return pl.pallas_call(
        pack_kernel,
        out_shape=jax.ShapeDtypeStruct((4, n + parts.shape[1], width), BF16),
        compiler_params=params(),
        cost_estimate=cost(0, 1),
        name="pack",
    )(grad, parts)


def fold_kernel(got, out):
    total = got[0, TILE:].astype(F32)
    for i in range(1, 4):
        total = total + got[i, TILE:].astype(F32)
    for i in range(4):
        out[TILE * i : TILE * (i + 1)] = got[i, :TILE]
    out[4 * TILE :] = total.astype(BF16)


def fold(got):
    extra, width = got.shape[1] - TILE, got.shape[2]
    return pl.pallas_call(
        fold_kernel,
        out_shape=jax.ShapeDtypeStruct((4 * TILE + extra, width), BF16),
        compiler_params=params(),
        cost_estimate=cost(0, 1),
        name="fold",
    )(got)


def collect_kernel(where, stays, first, second, two, out, slices):
    y = where[1]
    rows = 4 * TILE
    for k, line in zip(distances(where[2]), (stays, two, first, second)):
        out[pl.ds(pl.multiple_of(rows * k, rows), rows)] = line[:rows]
        slices[(y - k) & 3] = line[rows:].astype(F32)
    out[4 * rows :] = ((slices[0] + slices[1]) + (slices[2] + slices[3])).astype(BF16)


def collect(where, lines):
    rows, width = lines[0].shape
    extra = rows - 4 * TILE
    return pl.pallas_call(
        collect_kernel,
        out_shape=jax.ShapeDtypeStruct((HALF * TILE + extra, width), BF16),
        in_specs=[smem()] + [vmem()] * 4,
        out_specs=vmem(),
        scratch_shapes=[pltpu.VMEM((4, extra, width), F32)],
        compiler_params=params(),
        cost_estimate=cost(0, 3),
        name="collect",
    )(where, *lines)


def backward_half(other, where, rows, cols, v, grads, slots, acc):
    y, core, x = where[1], where[2], where[4]

    def source(s):
        r = rows[0, 0, s]
        at = ((y - ((r >> 1) & 3)) & 3) * 4 + (r >> 3)
        return grads[pl.ds(pl.multiple_of(at * TILE, TILE), TILE)]

    def target(s):
        c = cols[0, 0, s]
        return (((c & 3) - x) & 3) * 4 + (c >> 2)

    add_products(
        core ^ other, where, rows, slots, lambda i: None, lambda s: v[s], source, target, acc
    )


def first_kernel(where, rows, cols, v, grads, out, slots, acc):
    acc[...] = jnp.zeros_like(acc)
    backward_half(0, where, rows, cols, v, grads, slots, acc)
    out[...] = acc[:HALF]


def second_kernel(where, rows, cols, v, grads, mine, start, o0, o1, o2, o3, slots, acc):
    acc[:HALF] = start[...]
    acc[HALF] = jnp.zeros_like(acc[HALF])
    backward_half(1, where, rows, cols, v, grads, slots, acc)
    rest = HALF * TILE
    part = (mine[rest:].astype(F32) + grads[rest:].astype(F32)).astype(BF16)
    for k, out in zip(distances(where[2]), (o0, o1, o2, o3)):
        for i in range(4):
            out[TILE * i : TILE * (i + 1)] = acc[4 * k + i].astype(BF16)
        out[4 * TILE :] = part


def backward(where, rows, cols, v, mine, theirs):
    extra, width = mine.shape[0] - HALF * TILE, mine.shape[1]
    scratch = list_and_sums(width)
    work = cost(2 * 64 * TILE * TILE * width, 8)
    first = pl.pallas_call(
        first_kernel,
        out_shape=jax.ShapeDtypeStruct((HALF, TILE, width), F32),
        in_specs=[smem()] * 3 + [vmem()] * 2,
        out_specs=vmem(),
        scratch_shapes=scratch,
        compiler_params=params(),
        cost_estimate=work,
        name="first",
    )(where, rows, cols, v, mine)
    return pl.pallas_call(
        second_kernel,
        out_shape=(jax.ShapeDtypeStruct((4 * TILE + extra, width), BF16),) * 4,
        in_specs=[smem()] * 3 + [vmem()] * 4,
        out_specs=(vmem(),) * 4,
        scratch_shapes=scratch,
        compiler_params=params(),
        cost_estimate=work,
        name="second",
    )(where, rows, cols, v, theirs, mine, first)

def merge_kernel(where, p0, p1, p2, p3, out):
    x = where[4]
    parts = (p0, p1, p2, p3)
    extra = p0.shape[0] - 4 * TILE
    for i in range(4):
        block = slice(TILE * i, TILE * (i + 1))
        total = p0[block].astype(F32)
        for part in parts[1:]:
            total = total + part[block].astype(F32)
        out[i, :TILE] = total.astype(BF16)
        for k, part in zip(distances(where[2]), parts):
            at = pl.multiple_of(TILE + ((x - k) & 3) * extra, extra)
            out[i, pl.ds(at, extra)] = part[4 * TILE :]


def merge(where, parts):
    rows, width = parts[0].shape
    return pl.pallas_call(
        merge_kernel,
        out_shape=jax.ShapeDtypeStruct((4, TILE + 4 * (rows - 4 * TILE), width), BF16),
        in_specs=[smem()] + [vmem()] * 4,
        out_specs=vmem(),
        compiler_params=params(),
        cost_estimate=cost(0, 2),
        name="merge",
    )(where, *parts)


def last_kernel(scale, got, w, grad_out, weight_out):
    total = got[0, :TILE].astype(F32)
    for i in range(1, 4):
        total = total + got[i, :TILE].astype(F32)
    grad_out[...] = lax.dot_general(
        total.astype(BF16), w[...], (((1,), (1,)), ((), ())), preferred_element_type=F32
    ).astype(BF16)
    extra = got.shape[1] - TILE
    for i in range(4):
        weight_out[extra * i : extra * (i + 1)] = got[i, TILE:].astype(F32) * scale


def last(got, w, scale):
    width = w.shape[0]
    return pl.pallas_call(
        functools.partial(last_kernel, scale),
        out_shape=(
            jax.ShapeDtypeStruct((TILE, width), BF16),
            jax.ShapeDtypeStruct((width, width), F32),
        ),
        compiler_params=params(),
        cost_estimate=cost(2 * TILE * width * width, 1),
        name="last",
    )(got, w)


def shards(features, weight, tile_values, tile_rows, tile_cols, tile_count, cotangent):
    node_dev = features.shape[0]
    grad_scale = 1.0 / math.sqrt(node_dev * lax.axis_size("row") * lax.axis_size("col"))
    r, c = lax.axis_index("row"), lax.axis_index("col")
    where = jnp.stack([c >> 3, (c >> 1) & 3, c & 1, tile_count[0, 0], r & 3]).astype(jnp.int32)

    features, where = lax.optimization_barrier((features, where))
    xs = trade_row(jnp.broadcast_to(features[None], (ROWS,) + features.shape))
    xs, where = lax.optimization_barrier((xs, where))
    block = (where, tile_rows, tile_cols)
    got = send_core(forward(1, *block, tile_values, xs))
    keep = forward(0, *block, tile_values, xs)
    stays, two, first, second = pair(where, keep, got)
    got = [stays, send_y(two, TWO), send_y(first, FIRST), send_y(second, SECOND)]
    got = [v.astype(F32) for v in got]
    rows = (got[0] + got[1] + got[2] + got[3]).astype(BF16)
    turned = turn_tiles(where, tile_values)
    rows, turned = lax.optimization_barrier((rows, turned))
    activated, grad_pre, part = middle(trade_zh(rows), weight, cotangent)

    line = fold(trade_zh(pack(grad_pre, trade_row(part))))
    mine = collect(where, [line] + [send_y(line, which) for which in (FIRST, SECOND, TWO)])
    stays, two, first, second = backward(*block, turned, mine, send_core(mine))
    spread = [stays, send_x(two, TWO), send_x(first, FIRST), send_x(second, SECOND)]
    grad_features, grad_weight = last(trade_zl(merge(where, spread)), weight, grad_scale)
    return (activated, grad_features, grad_weight)


def solution(mesh):
    return jax.shard_map(
        shards,
        mesh=mesh,
        in_specs=(
            P(("col", "row"), None),
            P(),
            P("row", "col", None, None, None),
            P("row", "col", None),
            P("row", "col", None),
            P("row", "col"),
            P(("row", "col"), None),
        ),
        out_specs=(P(("row", "col"), None), P(("col", "row"), None), P()),
        check_vma=False,
    )
```

```python
import functools
import math

import jax
import jax.numpy as jnp
from jax import lax
from jax.experimental import pallas as pl
from jax.experimental.pallas import tpu as pltpu
from jax.sharding import PartitionSpec as P

TILE = 128
ROWS = 16
COLS = 32
HALF = 16
GROUP = 16
CHUNK = 16
SLOTS = 128
ROW, COL, PLACE = 0, 1, 2
VMEM_LIMIT = 24 * 1024 * 1024
BF16 = jnp.bfloat16
F32 = jnp.float32


FIRST, SECOND, TWO = 0, 1, 2


def distance(which, core):
    return 2 if which == TWO else 1 + 2 * (core ^ which)


def send_y(v, which):
    pairs = []
    for c in range(COLS):
        zh, y, core = c // 8, (c // 2) % 4, c % 2
        pairs.append((c, zh * 8 + (y + distance(which, core)) % 4 * 2 + core))
    return lax.ppermute(v, "col", pairs)


def send_x(v, which):
    pairs = []
    for r in range(ROWS):
        for c in range(COLS):
            to = r // 4 * 4 + (r + distance(which, c % 2)) % 4
            pairs.append((r * COLS + c, to * COLS + c))
    return lax.ppermute(v, ("row", "col"), pairs)


def send_core(v):
    return lax.ppermute(v, "col", [(c, c ^ 1) for c in range(COLS)])


def trade_row(v):
    return lax.all_to_all(v, "row", 0, 0)


def trade_zl(v):
    groups = [[zl * 4 + x for zl in range(4)] for x in range(4)]
    return lax.all_to_all(v, "row", 0, 0, axis_index_groups=groups)


def trade_zh(v):
    groups = [[zh * 8 + rest for zh in range(4)] for rest in range(8)]
    return lax.all_to_all(v, "col", 0, 0, axis_index_groups=groups)


def smem():
    return pl.BlockSpec(memory_space=pltpu.SMEM)


def vmem():
    return pl.BlockSpec(memory_space=pltpu.VMEM)


def params():
    return pltpu.CompilerParams(vmem_limit_bytes=VMEM_LIMIT)


def cost(flops, mib):
    return pl.CostEstimate(flops=flops, bytes_accessed=mib * 1024 * 1024, transcendentals=0)


def choose_slots(parity, block, slots, first, found):
    for u in range(CHUNK):
        s = first + u
        slots[found] = s
        chosen = ((block[ROW, s] & 1) == parity) & (s < block[PLACE, 3])
        found = found + jnp.where(chosen, 1, 0)
    return found


def add_products(parity, block, slots, arrive, tile, source, target, acc):
    def group(found, first):
        products, targets = [], []
        for u in range(GROUP):
            at = first + u
            s = jnp.where(at < found, slots[at], 0)
            targets.append(jnp.where(at < found, target(s), HALF))
            products.append(jnp.dot(tile(s), source(s), preferred_element_type=F32))
        for u in range(GROUP):
            acc[targets[u]] = acc[targets[u]] + products[u]

    def chunk(i, state):
        found, done = state
        arrive(i)
        found = choose_slots(parity, block, slots, i * CHUNK, found)
        full = (found - done) >= GROUP
        pl.when(full)(lambda: group(found, done))
        return found, jnp.where(full, done + GROUP, done)

    chunks = (block[PLACE, 3] + CHUNK - 1) // CHUNK
    found, done = lax.fori_loop(0, chunks, chunk, (jnp.int32(0), jnp.int32(0)))
    pl.when(done < found)(lambda: group(found, done))


def distances(core):
    return (0, 2, 1 + 2 * core, 3 - 2 * core)


def pair_kernel(block, a, b, *outs):
    for k, out in zip(distances(block[PLACE, 2]), outs):
        span = pl.ds(4 * k, 4)
        out[...] = (a[span].astype(F32) + b[span].astype(F32)).astype(BF16)


def pair(table, a, b):
    quarter = jax.ShapeDtypeStruct((4,) + a.shape[1:], BF16)
    return pl.pallas_call(
        pair_kernel,
        out_shape=(quarter,) * 4,
        in_specs=[smem()] + [vmem()] * 2,
        out_specs=(vmem(),) * 4,
        compiler_params=params(),
        cost_estimate=cost(0, 4),
        name="pair",
    )(table, a, b)


def fetch_chunks(live, v, tiles, sems):
    def chunk(i):
        part = pl.ds(i * CHUNK, CHUNK)
        return pltpu.make_async_copy(v.at[0, 0, part], tiles.at[part], sems.at[i])

    for i in range(SLOTS // CHUNK):
        pl.when(i * CHUNK < live)(chunk(i).start)
    return chunk


def forward_kernel(other, block, v, xs, out, slots, acc, tiles, sems):
    y, core = block[PLACE, 1], block[PLACE, 2]
    chunks = fetch_chunks(block[PLACE, 3], v, tiles, sems)
    acc[...] = jnp.zeros_like(acc)

    def target(s):
        r = block[ROW, s]
        return ((((r >> 1) & 3) - y) & 3) * 4 + (r >> 3)

    add_products(
        core ^ other,
        block,
        slots,
        lambda i: chunks(i).wait(),
        lambda s: tiles[s],
        lambda s: xs[block[COL, s]],
        target,
        acc,
    )
    out[...] = acc[:HALF].astype(BF16)


def list_and_sums(width):
    return [
        pltpu.SMEM((SLOTS + GROUP,), jnp.int32),
        pltpu.VMEM((HALF + 1, TILE, width), F32),
    ]


def forward(other, block, values, xs):
    width = xs.shape[-1]
    return pl.pallas_call(
        functools.partial(forward_kernel, other),
        out_shape=jax.ShapeDtypeStruct((HALF, TILE, width), BF16),
        in_specs=[smem()] + [pl.BlockSpec(memory_space=pltpu.HBM), vmem()],
        out_specs=vmem(),
        scratch_shapes=[
            *list_and_sums(width),
            pltpu.VMEM((SLOTS, TILE, TILE), BF16),
            pltpu.SemaphoreType.DMA((SLOTS // CHUNK,)),
        ],
        compiler_params=pltpu.CompilerParams(vmem_limit_bytes=50 * 1024 * 1024),
        cost_estimate=cost(2 * 64 * TILE * TILE * width, 7),
        name="forward",
    )(block, values, xs)


def turn_kernel(block, v, out, tiles, sems):
    chunks = fetch_chunks(block[PLACE, 3], v, tiles, sems)

    def step(i, _):
        chunks(i).wait()
        for u in range(CHUNK):
            out[i * CHUNK + u] = tiles[i * CHUNK + u].T
        return 0

    lax.fori_loop(0, (block[PLACE, 3] + CHUNK - 1) // CHUNK, step, 0)


def turn_tiles(block, v):
    shape = v.shape[2:]
    return pl.pallas_call(
        turn_kernel,
        out_shape=jax.ShapeDtypeStruct(shape, v.dtype),
        in_specs=[smem(), pl.BlockSpec(memory_space=pltpu.HBM)],
        out_specs=vmem(),
        scratch_shapes=[
            pltpu.VMEM(shape, v.dtype),
            pltpu.SemaphoreType.DMA((SLOTS // CHUNK,)),
        ],
        compiler_params=pltpu.CompilerParams(vmem_limit_bytes=46 * 1024 * 1024),
        cost_estimate=cost(0, 10),
        name="turn",
    )(block, v)


def middle_kernel(got, w, cot, act_out, grad_out, part_out):
    total = got[0].astype(F32)
    for i in range(1, 4):
        total = total + got[i].astype(F32)
    aggregated = total.astype(BF16)
    pre = jnp.dot(aggregated, w[...], preferred_element_type=F32)
    s = jax.nn.sigmoid(pre)
    act_out[...] = (pre * s).astype(BF16)
    grad = (cot[...].astype(F32) * (s * (1.0 + pre * (1.0 - s)))).astype(BF16)
    grad_out[...] = grad
    part = lax.dot_general(aggregated, grad, (((0,), (0,)), ((), ())), preferred_element_type=F32)
    part_out[...] = part.reshape(part_out.shape).astype(BF16)


def middle(got, w, cot):
    n, width = cot.shape
    rows = jax.ShapeDtypeStruct((n, width), BF16)
    return pl.pallas_call(
        middle_kernel,
        out_shape=(rows, rows, jax.ShapeDtypeStruct((ROWS, width // ROWS, width), BF16)),
        compiler_params=params(),
        cost_estimate=cost(4 * n * width * width, 1),
        name="middle",
    )(got, w, cot)


def pack_kernel(grad, parts, out):
    total = parts[0].astype(F32)
    for i in range(1, ROWS):
        total = total + parts[i].astype(F32)
    part = total.astype(BF16)
    for i in range(4):
        out[i, :TILE] = grad[...]
        out[i, TILE:] = part


def pack(grad, parts):
    n, width = grad.shape
    return pl.pallas_call(
        pack_kernel,
        out_shape=jax.ShapeDtypeStruct((4, n + parts.shape[1], width), BF16),
        compiler_params=params(),
        cost_estimate=cost(0, 1),
        name="pack",
    )(grad, parts)


def fold_kernel(got, out):
    total = got[0, TILE:].astype(F32)
    for i in range(1, 4):
        total = total + got[i, TILE:].astype(F32)
    for i in range(4):
        out[TILE * i : TILE * (i + 1)] = got[i, :TILE]
    out[4 * TILE :] = total.astype(BF16)


def fold(got):
    extra, width = got.shape[1] - TILE, got.shape[2]
    return pl.pallas_call(
        fold_kernel,
        out_shape=jax.ShapeDtypeStruct((4 * TILE + extra, width), BF16),
        compiler_params=params(),
        cost_estimate=cost(0, 1),
        name="fold",
    )(got)


def collect_kernel(block, stays, first, second, two, out, slices):
    y = block[PLACE, 1]
    rows = 4 * TILE
    for k, line in zip(distances(block[PLACE, 2]), (stays, two, first, second)):
        out[pl.ds(pl.multiple_of(rows * k, rows), rows)] = line[:rows]
        slices[(y - k) & 3] = line[rows:].astype(F32)
    out[4 * rows :] = ((slices[0] + slices[1]) + (slices[2] + slices[3])).astype(BF16)


def collect(block, lines):
    rows, width = lines[0].shape
    extra = rows - 4 * TILE
    return pl.pallas_call(
        collect_kernel,
        out_shape=jax.ShapeDtypeStruct((HALF * TILE + extra, width), BF16),
        in_specs=[smem()] + [vmem()] * 4,
        out_specs=vmem(),
        scratch_shapes=[pltpu.VMEM((4, extra, width), F32)],
        compiler_params=params(),
        cost_estimate=cost(0, 3),
        name="collect",
    )(block, *lines)


def backward_half(other, block, v, grads, slots, acc):
    y, core, x = block[PLACE, 1], block[PLACE, 2], block[PLACE, 4]

    def source(s):
        r = block[ROW, s]
        at = ((y - ((r >> 1) & 3)) & 3) * 4 + (r >> 3)
        return grads[pl.ds(pl.multiple_of(at * TILE, TILE), TILE)]

    def target(s):
        c = block[COL, s]
        return (((c & 3) - x) & 3) * 4 + (c >> 2)

    add_products(
        core ^ other, block, slots, lambda i: None, lambda s: v[s], source, target, acc
    )


def first_kernel(block, v, grads, out, slots, acc):
    acc[...] = jnp.zeros_like(acc)
    backward_half(0, block, v, grads, slots, acc)
    out[...] = acc[:HALF]


def second_kernel(block, v, grads, mine, start, o0, o1, o2, o3, slots, acc):
    acc[:HALF] = start[...]
    acc[HALF] = jnp.zeros_like(acc[HALF])
    backward_half(1, block, v, grads, slots, acc)
    rest = HALF * TILE
    part = (mine[rest:].astype(F32) + grads[rest:].astype(F32)).astype(BF16)
    for k, out in zip(distances(block[PLACE, 2]), (o0, o1, o2, o3)):
        for i in range(4):
            out[TILE * i : TILE * (i + 1)] = acc[4 * k + i].astype(BF16)
        out[4 * TILE :] = part


def backward(block, v, mine, theirs):
    extra, width = mine.shape[0] - HALF * TILE, mine.shape[1]
    scratch = list_and_sums(width)
    work = cost(2 * 64 * TILE * TILE * width, 8)
    first = pl.pallas_call(
        first_kernel,
        out_shape=jax.ShapeDtypeStruct((HALF, TILE, width), F32),
        in_specs=[smem()] + [vmem()] * 2,
        out_specs=vmem(),
        scratch_shapes=scratch,
        compiler_params=params(),
        cost_estimate=work,
        name="first",
    )(block, v, mine)
    return pl.pallas_call(
        second_kernel,
        out_shape=(jax.ShapeDtypeStruct((4 * TILE + extra, width), BF16),) * 4,
        in_specs=[smem()] + [vmem()] * 4,
        out_specs=(vmem(),) * 4,
        scratch_shapes=scratch,
        compiler_params=params(),
        cost_estimate=work,
        name="second",
    )(block, v, theirs, mine, first)

def merge_kernel(block, p0, p1, p2, p3, out):
    x = block[PLACE, 4]
    parts = (p0, p1, p2, p3)
    extra = p0.shape[0] - 4 * TILE
    for i in range(4):
        span = slice(TILE * i, TILE * (i + 1))
        total = p0[span].astype(F32)
        for part in parts[1:]:
            total = total + part[span].astype(F32)
        out[i, :TILE] = total.astype(BF16)
        for k, part in zip(distances(block[PLACE, 2]), parts):
            at = pl.multiple_of(TILE + ((x - k) & 3) * extra, extra)
            out[i, pl.ds(at, extra)] = part[4 * TILE :]


def merge(block, parts):
    rows, width = parts[0].shape
    return pl.pallas_call(
        merge_kernel,
        out_shape=jax.ShapeDtypeStruct((4, TILE + 4 * (rows - 4 * TILE), width), BF16),
        in_specs=[smem()] + [vmem()] * 4,
        out_specs=vmem(),
        compiler_params=params(),
        cost_estimate=cost(0, 2),
        name="merge",
    )(block, *parts)


def last_kernel(scale, got, w, grad_out, weight_out):
    total = got[0, :TILE].astype(F32)
    for i in range(1, 4):
        total = total + got[i, :TILE].astype(F32)
    grad_out[...] = lax.dot_general(
        total.astype(BF16), w[...], (((1,), (1,)), ((), ())), preferred_element_type=F32
    ).astype(BF16)
    extra = got.shape[1] - TILE
    for i in range(4):
        weight_out[extra * i : extra * (i + 1)] = got[i, TILE:].astype(F32) * scale


def last(got, w, scale):
    width = w.shape[0]
    return pl.pallas_call(
        functools.partial(last_kernel, scale),
        out_shape=(
            jax.ShapeDtypeStruct((TILE, width), BF16),
            jax.ShapeDtypeStruct((width, width), F32),
        ),
        compiler_params=params(),
        cost_estimate=cost(2 * TILE * width * width, 1),
        name="last",
    )(got, w)


def shards(features, weight, tile_values, tile_rows, tile_cols, tile_count, cotangent):
    node_dev = features.shape[0]
    grad_scale = 1.0 / math.sqrt(node_dev * lax.axis_size("row") * lax.axis_size("col"))
    r, c = lax.axis_index("row"), lax.axis_index("col")
    place = jnp.stack([c >> 3, (c >> 1) & 3, c & 1, tile_count[0, 0], r & 3]).astype(jnp.int32)
    place = jnp.pad(place, (0, SLOTS - place.shape[0]))
    block = jnp.concatenate([tile_rows[0], tile_cols[0], place[None]], axis=0)

    features, block = lax.optimization_barrier((features, block))
    xs = trade_row(jnp.broadcast_to(features[None], (ROWS,) + features.shape))
    xs, block = lax.optimization_barrier((xs, block))
    got = send_core(forward(1, block, tile_values, xs))
    keep = forward(0, block, tile_values, xs)
    stays, two, first, second = pair(block, keep, got)
    got = [stays, send_y(two, TWO), send_y(first, FIRST), send_y(second, SECOND)]
    got = [v.astype(F32) for v in got]
    rows = (got[0] + got[1] + got[2] + got[3]).astype(BF16)
    turned = turn_tiles(block, tile_values)
    rows, turned = lax.optimization_barrier((rows, turned))
    activated, grad_pre, part = middle(trade_zh(rows), weight, cotangent)

    line = fold(trade_zh(pack(grad_pre, trade_row(part))))
    mine = collect(block, [line] + [send_y(line, which) for which in (FIRST, SECOND, TWO)])
    stays, two, first, second = backward(block, turned, mine, send_core(mine))
    spread = [stays, send_x(two, TWO), send_x(first, FIRST), send_x(second, SECOND)]
    grad_features, grad_weight = last(trade_zl(merge(block, spread)), weight, grad_scale)
    return (activated, grad_features, grad_weight)


def solution(mesh):
    return jax.shard_map(
        shards,
        mesh=mesh,
        in_specs=(
            P(("col", "row"), None),
            P(),
            P("row", "col", None, None, None),
            P("row", "col", None),
            P("row", "col", None),
            P("row", "col"),
            P(("row", "col"), None),
        ),
        out_specs=(P(("row", "col"), None), P(("col", "row"), None), P()),
        check_vma=False,
    )
```
